32 devices in a mesh: groups: 2 (over y), rows: 16 (over z, x, core).
Axes of the slice: x: 2, y: 2, z: 4, core: 2. Of those that a mesh axis runs over, the one named last changes fastest.
Arguments:
- unary: float32 [64, 64, 2048], P(('groups', 'rows')), parts along dimension 0, may hold values from -300 to 8
- features: float32 [64, 5, 2048], P(('groups', 'rows')), parts along dimension 0, may hold values from -2 to 2
- compat: float32 [64, 64], replicated, may hold values from -4 to 4
- pairs: int32 [3, 128], P(None, ('groups', 'rows')), parts along dimension 1, may hold values from 0 to 2, as said below
- pair_count: int32 [32], P(('groups', 'rows')), parts along dimension 0, may hold values from 1 to 4, as said below
Outputs:
- probs: float32 [64, 64, 2048], P(('groups', 'rows')), parts along dimension 0
The draws below stay inside these ranges and needn't reach their ends.
There are 2 independent parts, one for each index of `groups`. The reference program is written for one: setup_inputs(seed, part) draws one part's arguments, and reference() takes and returns one part's arrays. A program takes and returns all parts, laid end to end along the dimension named above; an argument that names none is the same for every part. Nothing has to cross between parts.
Inputs may be any that keep to these rules, and one draw needn't show every extreme that they name: `pairs`: row 0 of a slot is the own local block, row 1 how many devices further along rows the partner block lies (0 to 2, never past the last device), row 2 the partner's local block there; on the same device the partner is another block than the own one. `pair_count`: some device has all 4 slots live.
All inputs are finite; a program needn't handle non-finite values.
Results may differ from the reference program's by a relative error of at most 0.0003.
Values may be sent and summed in bfloat16 or wider, within the bound.
No kernel may reach another device: no remote copies, remote signals or barrier semaphores. Data moves between devices by JAX's collectives and lax.ppermute only.
A program may use at most 192 MiB of HBM per device.

```python
import jax
import jax.numpy as jnp
from jax import lax

C = 64
P_SIZE = 2048
BLK_DEV = 2
SLOTS = 4
REACH = 2
ITERS = 2
NBLK = 32


def draw_unary(key, part):
    key = jax.random.fold_in(key, 3)
    return jnp.clip(2.0 * jax.random.normal(key, (NBLK, C, P_SIZE), jnp.float32), -8.0, 8.0)


def grid_positions(across_count):
    down_count = P_SIZE // across_count
    index = jnp.arange(P_SIZE, dtype=jnp.int32)
    across = (index % across_count).astype(jnp.float32) * (4.0 / max(across_count - 1, 1)) - 2.0
    down = (index // across_count).astype(jnp.float32) * (4.0 / max(down_count - 1, 1)) - 2.0
    places = jnp.stack([across, down])
    return jnp.broadcast_to(places[None, :, :], (NBLK, 2, P_SIZE))


def draw_features(key, part):
    key = jax.random.fold_in(key, 5)
    keys = jax.random.split(key, 3)
    across_count = max(P_SIZE // 32, 4)
    places = grid_positions(across_count)
    segment = jax.random.randint(keys[0], (NBLK, 1, P_SIZE), 0, 16)
    palette = jax.random.uniform(keys[1], (NBLK, 3, 16), jnp.float32, -1.2, 1.2)
    colours = jnp.take_along_axis(palette, jnp.broadcast_to(segment, (NBLK, 3, P_SIZE)), axis=2)
    colours = colours + jax.random.uniform(keys[2], (NBLK, 3, P_SIZE), jnp.float32, -0.8, 0.8)
    return jnp.clip(jnp.concatenate([places, colours], axis=1), -2.0, 2.0)


def draw_pairs(key, part):
    key = jax.random.fold_in(key, 7)
    keys = jax.random.split(key, 4)
    devices = NBLK // BLK_DEV
    total = devices * SLOTS
    slot_dev = jnp.arange(total, dtype=jnp.int32) // SLOTS
    owners = jax.random.randint(keys[0], (total,), 0, BLK_DEV)
    most = jnp.minimum(REACH, devices - 1 - slot_dev)
    offsets = jax.random.randint(keys[1], (total,), 0, REACH + 1) % (most + 1)
    partners = jax.random.randint(keys[2], (total,), 0, BLK_DEV)
    other = (owners + 1 + jax.random.randint(keys[3], (total,), 0, BLK_DEV - 1)) % BLK_DEV
    partners = jnp.where(offsets == 0, other, partners)
    return jnp.stack([owners, offsets, partners]).astype(jnp.int32)


def draw_pair_count(key, part):
    key = jax.random.fold_in(key, 11)
    keys = jax.random.split(key, 2)
    devices = NBLK // BLK_DEV
    counts = jax.random.randint(keys[0], (devices,), SLOTS // 4, SLOTS + 1)
    fullest = jax.random.randint(keys[1], (), 0, devices)
    return jnp.where(jnp.arange(devices) == fullest, SLOTS, counts).astype(jnp.int32)


def centred(rng, shape, scale, most, held_as=jnp.bfloat16):
    return jnp.clip(scale * jax.random.normal(rng, shape, jnp.float32), -most, most).astype(held_as)


def setup_inputs(seed: int = 0, part: int = 0) -> dict:
    key_list = jax.random.split(jax.random.key(seed), 6)
    own_keys = jax.random.split(jax.random.fold_in(key_list[5], part), 6)
    return {
        "unary": draw_unary(jax.random.fold_in(jax.random.fold_in(key_list[5], part), 71), part),
        "features": draw_features(jax.random.fold_in(jax.random.fold_in(key_list[5], part), 71), part),
        "compat": centred(key_list[2], (C, C), 1.0, 4.0, jnp.float32),
        "pairs": draw_pairs(jax.random.fold_in(jax.random.fold_in(key_list[5], part), 71), part),
        "pair_count": draw_pair_count(jax.random.fold_in(jax.random.fold_in(key_list[5], part), 71), part),
    }


def square_dist(feat_own, feat_part):
    dist = jnp.zeros((feat_own.shape[1], feat_part.shape[1]), jnp.float32)
    for index in range(feat_own.shape[0]):
        spread = feat_own[index][:, None] - feat_part[index][None, :]
        dist = dist + spread * spread
    return dist


def pair_kernel(feat_own, feat_part, alive):
    dist = square_dist(feat_own, feat_part)
    return jnp.where(alive, jnp.exp(-0.5 * dist), 0.0).astype(jnp.bfloat16)


def self_kernel(feat):
    dist = square_dist(feat, feat)
    width = feat.shape[1]
    diagonal = jnp.arange(width)[:, None] == jnp.arange(width)[None, :]
    return jnp.where(diagonal, 0.0, jnp.exp(-0.5 * dist)).astype(jnp.bfloat16)


def self_message(items):
    prob_wide, feat = items
    kernel = self_kernel(feat).astype(jnp.float32)
    return jnp.einsum('cj,ij->ci', prob_wide, kernel)


def reference(unary, features, compat, pairs, pair_count):
    msg_scale = 16.0 / P_SIZE
    total = pairs.shape[1]
    slot_ids = jnp.arange(total, dtype=jnp.int32)
    slot_dev = slot_ids // SLOTS
    owner_glob = (slot_dev * BLK_DEV + pairs[0]).astype(jnp.int32)
    partner_glob = ((slot_dev + pairs[1]) * BLK_DEV + pairs[2]).astype(jnp.int32)
    alive = (slot_ids % SLOTS) < pair_count[slot_dev]
    probs = jax.nn.softmax(-unary, axis=1)
    for step in range(ITERS):
        prob_low = probs.astype(jnp.bfloat16)
        prob_wide = prob_low.astype(jnp.float32)
        message = lax.map(self_message, (prob_wide, features))

        def visit(carry, index):
            owner = owner_glob[index]
            partner = partner_glob[index]
            kernel = pair_kernel(features[owner], features[partner], alive[index]).astype(jnp.float32)
            carry = carry.at[owner].add(jnp.einsum('cj,ij->ci', prob_wide[partner], kernel))
            carry = carry.at[partner].add(jnp.einsum('ci,ij->cj', prob_wide[owner], kernel))
            return carry, None

        message, unused = lax.scan(visit, message, slot_ids)
        pairwise = jnp.einsum('ce,bep->bcp', compat, message, precision=lax.Precision.HIGHEST) * msg_scale
        probs = jax.nn.softmax(-unary - pairwise, axis=1)
    return probs
```

```python
import functools

import jax
import jax.numpy as jnp
from jax import lax
from jax.experimental import pallas as pl
from jax.experimental.pallas import tpu as pltpu
from jax.sharding import PartitionSpec as P

ITERS = 2
FEATS = 5
PART_ROWS = 16
META = 3 * FEATS
DEPTH = 4 * PART_ROWS
TILES = 2
LOG2E = 1.4426950408889634
F32 = jnp.float32
BF16 = jnp.bfloat16
VMEM = pl.BlockSpec(memory_space=pltpu.VMEM)
SMEM = pl.BlockSpec(memory_space=pltpu.SMEM)
ANY = pl.BlockSpec(memory_space=pl.ANY)
PARAMS = pltpu.CompilerParams(vmem_limit_bytes=44 * 2**20)


def split3(value):
    high = value.astype(BF16)
    rest = value - high.astype(F32)
    middle = rest.astype(BF16)
    low = (rest - middle.astype(F32)).astype(BF16)
    return high, middle, low


def softmax(scores):
    shifted = jnp.exp(scores - jnp.max(scores, axis=0, keepdims=True))
    return shifted / jnp.sum(shifted, axis=0, keepdims=True)


def small_dot(left, right):
    return jnp.dot(left, right, preferred_element_type=F32)


def slot_code(pairs_ref, slot):
    return pairs_ref[0, slot] * 6 + pairs_ref[1, slot] * 2 + pairs_ref[2, slot]


def norm_parts(values):
    norm = jnp.sum(values * values, axis=0, keepdims=True) * (-0.5 * LOG2E)
    return [part.astype(F32) for part in split3(norm)]


def prep_body(unary_ref, feat_ref, pairs_ref, count_ref, payload_ref, right_ref):
    blocks, classes, pixels = unary_ref.shape
    slots = pairs_ref.shape[1]
    row = lax.broadcasted_iota(jnp.int32, (PART_ROWS, 8), 0)
    col = lax.broadcasted_iota(jnp.int32, (PART_ROWS, 8), 1)
    place = [
        jnp.where((row == col + FEATS * part) & (col < FEATS), 1.0, 0.0).astype(BF16)
        for part in range(3)
    ]
    spread = place[0] + place[1] + place[2]
    wide_row = lax.broadcasted_iota(jnp.int32, (PART_ROWS, pixels), 0)
    wide_col = lax.broadcasted_iota(jnp.int32, (PART_ROWS, pixels), 1)
    meta = jnp.zeros((PART_ROWS, pixels), F32)
    for slot in range(slots):
        code = jnp.where(slot < count_ref[0], slot_code(pairs_ref, slot), -1)
        meta = meta + jnp.where((wide_row == META) & (wide_col == code), 1.0, 0.0)
    for block in range(blocks):
        payload_ref[block, :classes, :] = softmax(-unary_ref[block]).astype(BF16)
        values = feat_ref[block]
        parts = split3(values)
        own = meta
        for part in range(3):
            own = own + small_dot(place[part], parts[part])
        payload_ref[block, classes:, :] = own.astype(BF16)
        for index, part in enumerate(split3(values * LOG2E)):
            right_ref[block, index * PART_ROWS : (index + 1) * PART_ROWS, :] = small_dot(
                spread, part
            ).astype(BF16)
        high, middle, low = norm_parts(values)
        norms = jnp.where(wide_row < 3, 1.0, 0.0)
        for index, part in enumerate((high, middle, low)):
            norms = jnp.where(wide_row == 3 + index, part, norms)
        right_ref[block, 3 * PART_ROWS :, :] = norms.astype(BF16)


def prep(unary, feats, pairs, pair_count):
    blocks, classes, pixels = unary.shape
    return pl.pallas_call(
        prep_body,
        out_shape=(
            jax.ShapeDtypeStruct((blocks, classes + PART_ROWS, pixels), BF16),
            jax.ShapeDtypeStruct((blocks, DEPTH, pixels), BF16),
        ),
        in_specs=[VMEM, VMEM, SMEM, SMEM],
        out_specs=(VMEM, VMEM),
        compiler_params=PARAMS,
        name="prep",
    )(unary, feats, pairs, pair_count)


def left_operand(payload_ref, block, classes):
    pixels = payload_ref.shape[2]
    own = payload_ref[block, classes:, :]
    row = lax.broadcasted_iota(jnp.int32, (8, PART_ROWS), 0)
    col = lax.broadcasted_iota(jnp.int32, (8, PART_ROWS), 1)
    gather = (row < FEATS) & ((col == row) | (col == row + FEATS) | (col == row + 2 * FEATS))
    values = small_dot(jnp.where(gather, 1.0, 0.0).astype(BF16), own)
    wide_row = lax.broadcasted_iota(jnp.int32, (PART_ROWS, pixels), 0)
    norms = jnp.where((wide_row >= 3) & (wide_row < 6), 1.0, 0.0)
    for index, part in enumerate(norm_parts(values)):
        norms = jnp.where(wide_row == index, part, norms)
    return jnp.concatenate([own, own, own, norms.astype(BF16)], axis=0).T


def meta_count(payload_ref, classes, lane):
    row = lax.broadcasted_iota(jnp.int32, (PART_ROWS, 128), 0)
    col = lax.broadcasted_iota(jnp.int32, (PART_ROWS, 128), 1)
    own = payload_ref[0, classes:, :128].astype(F32)
    return jnp.sum(jnp.where((row == META) & (col == lane), own, 0.0)).astype(jnp.int32)


def finish(unary_ref, compat_ref, message, block):
    scale = 16.0 / unary_ref.shape[2]
    pairwise = jnp.dot(
        compat_ref[...], message, precision=lax.Precision.HIGHEST, preferred_element_type=F32
    )
    return softmax(-unary_ref[block] - pairwise * scale)


def build_body(count_src, base, first, last, *refs):
    refs = list(refs)
    offs_ref, pairs_ref, live_ref, right_ref = refs[:4]
    del refs[:4]
    sources = refs[:count_src]
    del refs[:count_src]
    if last:
        unary_ref, compat_ref = refs[:2]
        del refs[:2]
    if not first:
        total_in = refs[0]
        del refs[:2]
    total_ref, kernels_ref, mult_ref, left, tiles, sems, jobs, *rest = refs
    total = rest[0] if last else total_ref
    blocks, classes, pixels = total.shape
    slots = pairs_ref.shape[1]
    width = pixels // TILES
    local = first

    jobs[0] = 0
    for block in range(blocks):
        if local:
            total[block] = -sources[0][block, :classes, :].astype(F32)
        else:
            total[block] = total_in[block]

    def tile_copy(tile, slot):
        return pltpu.make_async_copy(
            tiles.at[tile], kernels_ref.at[slot, tile], sems.at[tile]
        )

    for source, payload_ref in enumerate(sources):
        offset = offs_ref[source]

        def multiplicity(block, target):
            ahead = jnp.int32(0)
            for slot in range(slots):
                hit = (
                    (slot < live_ref[0])
                    & (pairs_ref[0, slot] == target)
                    & (pairs_ref[1, slot] == offset)
                    & (pairs_ref[2, slot] == block)
                )
                ahead = ahead + jnp.where(hit, 1, 0)
            if local:
                for slot in range(slots):
                    hit = (
                        (slot < live_ref[0])
                        & (pairs_ref[0, slot] == block)
                        & (pairs_ref[1, slot] == 0)
                        & (pairs_ref[2, slot] == target)
                    )
                    ahead = ahead + jnp.where(hit, 1, 0)
                return jnp.where(block == target, 1, ahead)
            behind = meta_count(payload_ref, classes, block * 6 - offset * 2 + target)
            return jnp.where(offset > 0, ahead, behind)

        @pl.loop(0, blocks)
        def _(block):
            counts = [multiplicity(block, target) for target in range(blocks)]
            for target in range(blocks):
                mult_ref[source, block * blocks + target] = counts[target]

            @pl.when(sum(counts) > 0)
            def _():
                left[...] = left_operand(payload_ref, block, classes)

                @pl.loop(0, blocks)
                def _(target):
                    count = mult_ref[source, block * blocks + target]

                    @pl.when(count > 0)
                    def _():
                        scale = count.astype(F32)
                        slot = base + (source * blocks + block) * blocks + target
                        for tile in range(TILES):
                            @pl.when(jobs[0] > 0)
                            def _():
                                tile_copy(tile, slot).wait()

                            cut = slice(tile * width, (tile + 1) * width)
                            scores = jnp.dot(
                                left[...], right_ref[target, :, cut], preferred_element_type=F32
                            )
                            tiles[tile] = jnp.exp2(scores).astype(BF16)
                            tile_copy(tile, slot).start()
                            total[target, :, cut] += scale * jnp.dot(
                                payload_ref[block, :classes, :],
                                tiles[tile],
                                preferred_element_type=F32,
                            )
                        jobs[0] = jobs[0] + 1

    if last:
        for block in range(blocks):
            total_ref[block] = finish(unary_ref, compat_ref, total[block], block).astype(BF16)

    @pl.when(jobs[0] > 0)
    def _():
        for tile in range(TILES):
            tile_copy(tile, 0).wait()


def build(base, offs, pairs, live, right, sources, total, kernels, slots, ending=None):
    blocks, rows, pixels = sources[0].shape
    classes = rows - PART_ROWS
    first, last = total is None, ending is not None
    operands = [offs, pairs, live, right, *sources]
    specs = [SMEM, SMEM, SMEM, VMEM] + [VMEM] * len(sources)
    if last:
        operands += list(ending)
        specs += [VMEM, VMEM]
    aliases = {}
    if not first:
        aliases = {len(operands) + 1: 1}
        operands += [total, kernels]
        specs += [VMEM, ANY]
    width = pixels // TILES
    scratch = [
        pltpu.VMEM((pixels, DEPTH), BF16),
        pltpu.VMEM((TILES, pixels, width), BF16),
        pltpu.SemaphoreType.DMA((TILES,)),
        pltpu.SMEM((1,), jnp.int32),
    ]
    if last:
        scratch.append(pltpu.VMEM((blocks, classes, pixels), F32))
    work = len(sources) * 2 * pixels * pixels * 320
    return pl.pallas_call(
        functools.partial(build_body, len(sources), base, first, last),
        out_shape=(
            jax.ShapeDtypeStruct((blocks, classes, pixels), BF16 if last else F32),
            jax.ShapeDtypeStruct((slots, TILES, pixels, width), BF16),
            jax.ShapeDtypeStruct((len(sources), blocks * blocks), jnp.int32),
        ),
        in_specs=specs,
        out_specs=(VMEM, ANY, SMEM),
        scratch_shapes=scratch,
        input_output_aliases=aliases,
        compiler_params=PARAMS,
        cost_estimate=pl.CostEstimate(
            flops=2 * work, bytes_accessed=len(sources) * 2**24, transcendentals=0
        ),
        name="build",
    )(*operands)


def apply_body(count_src, bases, first, last, *refs):
    refs = list(refs)
    mults = refs[:count_src]
    sources = refs[count_src : 2 * count_src]
    del refs[: 2 * count_src]
    kernels_ref = refs.pop(0)
    if last:
        unary_ref, compat_ref = refs[:2]
        del refs[:2]
    if not first:
        total_in = refs.pop(0)
    out_ref, probs, tiles, sems, jobs, *rest = refs
    total = rest[0] if last else out_ref
    blocks, classes, pixels = total.shape
    width = pixels // TILES
    for block in range(blocks):
        if first:
            total[block] = -sources[0][block].astype(F32)
        else:
            total[block] = total_in[block]

    jobs[0, 0] = 0
    for source in range(count_src):
        for block in range(blocks):
            probs[source * blocks + block] = sources[source][block]
            for target in range(blocks):
                place = block * blocks + target
                count = mults[source][0, place]

                @pl.when(count > 0)
                def _():
                    entry = jobs[0, 0] + 1
                    jobs[0, 0] = entry
                    jobs[entry, 0] = bases[source] + place
                    jobs[entry, 1] = source * blocks + block
                    jobs[entry, 2] = target
                    jobs[entry, 3] = count

    number = jobs[0, 0]

    def fetch(job, tile):
        hold = lax.rem(job, 2) * TILES + tile
        return pltpu.make_async_copy(
            kernels_ref.at[jobs[job + 1, 0], tile], tiles.at[hold], sems.at[hold]
        )

    for job in range(2):
        @pl.when(job < number)
        def _():
            for tile in range(TILES):
                fetch(job, tile).start()

    @pl.loop(0, number)
    def _(job):
        scale = jobs[job + 1, 3].astype(F32)
        index = jobs[job + 1, 1]
        target = jobs[job + 1, 2]
        for tile in range(TILES):
            fetch(job, tile).wait()
            cut = slice(tile * width, (tile + 1) * width)
            total[target, :, cut] += scale * jnp.dot(
                probs[index],
                tiles[lax.rem(job, 2) * TILES + tile],
                preferred_element_type=F32,
            )

            @pl.when(job + 2 < number)
            def _():
                fetch(job + 2, tile).start()

    if last:
        for block in range(blocks):
            out_ref[block] = finish(unary_ref, compat_ref, total[block], block)


def apply(bases, mults, sources, kernels, total, ending=None):
    blocks, classes, pixels = sources[0].shape
    first, last = total is None, ending is not None
    number = len(sources)
    operands = [*mults, *sources, kernels]
    specs = [SMEM] * number + [VMEM] * number + [ANY]
    if last:
        operands += list(ending)
        specs += [VMEM, VMEM]
    if not first:
        operands.append(total)
        specs.append(VMEM)
    width = pixels // TILES
    scratch = [
        pltpu.VMEM((number * blocks, classes, pixels), BF16),
        pltpu.VMEM((2 * TILES, pixels, width), BF16),
        pltpu.SemaphoreType.DMA((2 * TILES,)),
        pltpu.SMEM((number * blocks * blocks + 1, 4), jnp.int32),
    ]
    if last:
        scratch.append(pltpu.VMEM((blocks, classes, pixels), F32))
    return pl.pallas_call(
        functools.partial(apply_body, number, bases, first, last),
        out_shape=jax.ShapeDtypeStruct((blocks, classes, pixels), F32),
        in_specs=specs,
        out_specs=VMEM,
        scratch_shapes=scratch,
        compiler_params=PARAMS,
        cost_estimate=pl.CostEstimate(
            flops=number * 2 * pixels * pixels * 64, bytes_accessed=number * 2**24, transcendentals=0
        ),
        name="apply",
    )(*operands)


def permute(value, place):
    count = lax.axis_size("rows")
    moves = [(index, place(index)) for index in range(count)]
    return lax.ppermute(value, "rows", [move for move in moves if 0 <= move[1] < count])


def other_core(value):
    return permute(value, lambda index: index ^ 1)


def even_pair(value):
    return permute(value, lambda index: index ^ 2)


def odd_pair(value):
    return permute(value, lambda index: ((index + 2) ^ 2) - 2)


def on_device(unary, features, compat, pairs, pair_count):
    blocks = unary.shape[0]
    group = blocks * blocks
    me = lax.axis_index("rows")
    core, side = me & 1, (me >> 1) & 1
    off_core = 1 - 2 * core
    off_even = 2 - 4 * side
    offsets = [jnp.zeros_like(off_core), off_core, off_even, -off_even, -off_core]
    offsets = [value.astype(jnp.int32).reshape(1) for value in offsets]
    feats = jnp.pad(features, ((0, 0), (0, 8 - FEATS), (0, 0)))
    payload, right = prep(unary, feats, pairs, pair_count)

    def exchange(value):
        core_value = other_core(value)
        even_value = even_pair(value)
        odd_value = odd_pair(value)
        far_value = other_core(jnp.where(core == side, even_value, odd_value))
        return [value, core_value, even_value, odd_value, far_value]

    window = exchange(payload)
    total, kernels = None, None
    mults = []
    for stage in range(5):
        ending = (unary, compat) if stage == 4 else None
        total, kernels, mult = build(
            stage * group, offsets[stage], pairs, pair_count, right, [window[stage]], total, kernels,
            5 * group, ending,
        )
        mults.append(mult)
    window = exchange(total)
    total = None
    for stages in ((0, 1), (2,), (3,), (4,)):
        ending = (unary, compat) if stages[-1] == 4 else None
        total = apply(
            [stage * group for stage in stages],
            [mults[stage] for stage in stages],
            [window[stage] for stage in stages],
            kernels,
            total,
            ending,
        )
    return total


def solution(mesh):
    placed = (
        P(("groups", "rows"), None, None),
        P(("groups", "rows"), None, None),
        P(),
        P(None, ("groups", "rows")),
        P(("groups", "rows")),
    )
    return jax.shard_map(
        on_device,
        mesh=mesh,
        in_specs=placed,
        out_specs=P(("groups", "rows"), None, None),
        check_vma=False,
    )
```

```python
import functools

import jax
import jax.numpy as jnp
from jax import lax
from jax.experimental import pallas as pl
from jax.experimental.pallas import tpu as pltpu
from jax.sharding import PartitionSpec as P

ITERS = 2
FEATS = 5
PART_ROWS = 16
META = 3 * FEATS
DEPTH = 4 * PART_ROWS
TILES = 2
PARTS = 2
LOG2E = 1.4426950408889634
F32 = jnp.float32
BF16 = jnp.bfloat16
VMEM = pl.BlockSpec(memory_space=pltpu.VMEM)
SMEM = pl.BlockSpec(memory_space=pltpu.SMEM)
ANY = pl.BlockSpec(memory_space=pl.ANY)
PARAMS = pltpu.CompilerParams(vmem_limit_bytes=30 * 2**20)
SMALL = pltpu.CompilerParams(vmem_limit_bytes=16 * 2**20)


def split3(value):
    high = value.astype(BF16)
    rest = value - high.astype(F32)
    middle = rest.astype(BF16)
    low = (rest - middle.astype(F32)).astype(BF16)
    return high, middle, low


def softmax(scores):
    shifted = jnp.exp(scores - jnp.max(scores, axis=0, keepdims=True))
    return shifted / jnp.sum(shifted, axis=0, keepdims=True)


def small_dot(left, right):
    return jnp.dot(left, right, preferred_element_type=F32)


def slot_of(info_ref, slots, slot):
    return [info_ref[part * slots + slot] for part in range(3)]


def slots_of(info_ref):
    return (info_ref.shape[0] - 6) // 3


def is_live(info_ref, slots, slot):
    return slot < info_ref[3 * slots]


def slot_code(info_ref, slots, slot):
    owner, offset, partner = slot_of(info_ref, slots, slot)
    return owner * 6 + offset * 2 + partner


def norm_parts(values):
    norm = jnp.sum(values * values, axis=0, keepdims=True) * (-0.5 * LOG2E)
    return [part.astype(F32) for part in split3(norm)]


def prep_body(unary_ref, feat_ref, info_ref, payload_ref, right_ref):
    blocks, classes, pixels = unary_ref.shape
    slots = slots_of(info_ref)
    row = lax.broadcasted_iota(jnp.int32, (PART_ROWS, 8), 0)
    col = lax.broadcasted_iota(jnp.int32, (PART_ROWS, 8), 1)
    place = [
        jnp.where((row == col + FEATS * part) & (col < FEATS), 1.0, 0.0).astype(BF16)
        for part in range(3)
    ]
    spread = place[0] + place[1] + place[2]
    wide_row = lax.broadcasted_iota(jnp.int32, (PART_ROWS, pixels), 0)
    wide_col = lax.broadcasted_iota(jnp.int32, (PART_ROWS, pixels), 1)
    feat_row = lax.broadcasted_iota(jnp.int32, (8, pixels), 0)
    meta = jnp.zeros((PART_ROWS, pixels), F32)
    for slot in range(slots):
        code = jnp.where(is_live(info_ref, slots, slot), slot_code(info_ref, slots, slot), -1)
        meta = meta + jnp.where((wide_row == META) & (wide_col == code), 1.0, 0.0)
    for block in range(blocks):
        payload_ref[block, :classes, :] = softmax(-unary_ref[block]).astype(BF16)
        values = jnp.zeros((8, pixels), F32)
        for feature in range(FEATS):
            values = jnp.where(feat_row == feature, feat_ref[feature, block : block + 1, :], values)
        parts = split3(values)
        own = meta
        for part in range(3):
            own = own + small_dot(place[part], parts[part])
        payload_ref[block, classes:, :] = own.astype(BF16)
        for index, part in enumerate(split3(values * LOG2E)):
            right_ref[block, index * PART_ROWS : (index + 1) * PART_ROWS, :] = small_dot(
                spread, part
            ).astype(BF16)
        high, middle, low = norm_parts(values)
        norms = jnp.where(wide_row < 3, 1.0, 0.0)
        for index, part in enumerate((high, middle, low)):
            norms = jnp.where(wide_row == 3 + index, part, norms)
        right_ref[block, 3 * PART_ROWS :, :] = norms.astype(BF16)


def prep(unary, feats, info):
    blocks, classes, pixels = unary.shape
    return pl.pallas_call(
        prep_body,
        out_shape=(
            jax.ShapeDtypeStruct((blocks, classes + PART_ROWS, pixels), BF16),
            jax.ShapeDtypeStruct((blocks, DEPTH, pixels), BF16),
        ),
        in_specs=[VMEM, VMEM, SMEM],
        out_specs=(VMEM, VMEM),
        compiler_params=SMALL,
        name="prep",
    )(unary, feats, info)


def left_operand(payload_ref, block, classes):
    pixels = payload_ref.shape[2]
    own = payload_ref[block, classes:, :]
    row = lax.broadcasted_iota(jnp.int32, (8, PART_ROWS), 0)
    col = lax.broadcasted_iota(jnp.int32, (8, PART_ROWS), 1)
    gather = (row < FEATS) & ((col == row) | (col == row + FEATS) | (col == row + 2 * FEATS))
    values = small_dot(jnp.where(gather, 1.0, 0.0).astype(BF16), own)
    wide_row = lax.broadcasted_iota(jnp.int32, (PART_ROWS, pixels), 0)
    norms = jnp.where((wide_row >= 3) & (wide_row < 6), 1.0, 0.0)
    for index, part in enumerate(norm_parts(values)):
        norms = jnp.where(wide_row == index, part, norms)
    return jnp.concatenate([own, own, own, norms.astype(BF16)], axis=0).T


def meta_counts(payload_ref, classes, blocks, offset):
    row = lax.broadcasted_iota(jnp.int32, (PART_ROWS, 128), 0)
    col = lax.broadcasted_iota(jnp.int32, (PART_ROWS, 128), 1)
    own = payload_ref[0, classes:, :128].astype(F32)
    weight = jnp.zeros((PART_ROWS, 128), F32)
    for block in range(blocks):
        for target in range(blocks):
            lane = block * 6 - offset * 2 + target
            step = 8.0 ** (block * blocks + target)
            weight = jnp.where((row == META) & (col == lane), step, weight)
    return jnp.sum(own * weight).astype(jnp.int32)


def finish(unary_ref, compat_ref, message, block):
    scale = 16.0 / unary_ref.shape[2]
    pairwise = jnp.dot(
        compat_ref[...], message, precision=lax.Precision.HIGHEST, preferred_element_type=F32
    )
    return softmax(-unary_ref[block] - pairwise * scale)


def build_body(stage, first, last, *refs):
    refs = list(refs)
    info_ref, right_ref = refs[:2]
    del refs[:2]
    sources = refs[: len(stage)]
    del refs[: len(stage)]
    if last:
        unary_ref, compat_ref = refs[:2]
        del refs[:2]
    if not first:
        total_in = refs[0]
        del refs[:2]
    total_ref, kernels_ref, mult_ref = refs[:3]
    del refs[:3]
    left, tiles, sems, jobs, *rest = refs
    total = rest[0] if last else total_ref
    blocks, classes, pixels = total.shape
    slots = slots_of(info_ref)
    width = pixels // TILES
    part_width = width // PARTS

    jobs[0] = 0
    for block in range(blocks):
        if first:
            total[block] = -sources[0][block, :classes, :].astype(F32)
        else:
            total[block] = total_in[block]

    def tile_copies(tile, slot):
        return [
            pltpu.make_async_copy(
                tiles.at[tile, :, pl.ds(part * part_width, part_width)],
                kernels_ref.at[slot, tile * PARTS + part],
                sems.at[tile, part],
            )
            for part in range(PARTS)
        ]

    for index, (source, payload_ref) in enumerate(zip(stage, sources)):
        offset = info_ref[3 * slots + 1 + source]
        packed = None if first else meta_counts(payload_ref, classes, blocks, offset)

        def multiplicity(block, target):
            ahead = jnp.int32(0)
            for slot in range(slots):
                live = is_live(info_ref, slots, slot)
                owner, distance, partner = slot_of(info_ref, slots, slot)
                hit = live & (owner == target) & (distance == offset) & (partner == block)
                ahead = ahead + jnp.where(hit, 1, 0)
                if first:
                    hit = live & (owner == block) & (distance == 0) & (partner == target)
                    ahead = ahead + jnp.where(hit, 1, 0)
            if first:
                return jnp.where(block == target, 1, ahead)
            behind = lax.shift_right_logical(packed, 3 * (block * blocks + target)) & 7
            return jnp.where(offset > 0, ahead, behind)

        @pl.loop(0, blocks)
        def _(block):
            counts = [multiplicity(block, target) for target in range(blocks)]
            for target in range(blocks):
                mult_ref[(index * blocks + block) * blocks + target] = counts[target]

            @pl.when(sum(counts) > 0)
            def _():
                left[...] = left_operand(payload_ref, block, classes)

                @pl.loop(0, blocks)
                def _(target):
                    place = block * blocks + target
                    count = mult_ref[index * blocks * blocks + place]

                    @pl.when(count > 0)
                    def _():
                        scale = count.astype(F32)
                        slot = source * blocks * blocks + place
                        for tile in range(TILES):
                            @pl.when(jobs[0] > 0)
                            def _():
                                for copy in tile_copies(tile, slot):
                                    copy.wait()

                            cut = slice(tile * width, (tile + 1) * width)
                            scores = jnp.dot(
                                left[...], right_ref[target, :, cut], preferred_element_type=F32
                            )
                            tiles[tile] = jnp.exp2(scores).astype(BF16)
                            for copy in tile_copies(tile, slot):
                                copy.start()
                            total[target, :, cut] += scale * jnp.dot(
                                payload_ref[block, :classes, :],
                                tiles[tile],
                                preferred_element_type=F32,
                            )
                        jobs[0] = jobs[0] + 1

    if last:
        for block in range(blocks):
            total_ref[block] = finish(unary_ref, compat_ref, total[block], block).astype(BF16)

    @pl.when(jobs[0] > 0)
    def _():
        for tile in range(TILES):
            for copy in tile_copies(tile, 0):
                copy.wait()


def build(stage, info, right, sources, total, kernels, slots, ending):
    blocks, rows, pixels = sources[0].shape
    classes = rows - PART_ROWS
    first, last = total is None, ending is not None
    operands = [info, right, *sources]
    specs = [SMEM, VMEM] + [VMEM] * len(sources)
    if last:
        operands += list(ending)
        specs += [VMEM, VMEM]
    aliases = {}
    if not first:
        aliases = {len(operands) + 1: 1}
        operands += [total, kernels]
        specs += [VMEM, ANY]
    width = pixels // TILES
    outs = [
        jax.ShapeDtypeStruct((blocks, classes, pixels), BF16 if last else F32),
        jax.ShapeDtypeStruct((slots, TILES * PARTS, pixels, width // PARTS), BF16),
        jax.ShapeDtypeStruct((len(sources) * blocks * blocks,), jnp.int32),
    ]
    out_specs = [VMEM, ANY, SMEM]
    scratch = [
        pltpu.VMEM((pixels, DEPTH), BF16),
        pltpu.VMEM((TILES, pixels, width), BF16),
        pltpu.SemaphoreType.DMA((TILES, PARTS)),
        pltpu.SMEM((1,), jnp.int32),
    ]
    if last:
        scratch.append(pltpu.VMEM((blocks, classes, pixels), F32))
    work = len(sources) * 2 * pixels * pixels * 320
    return pl.pallas_call(
        functools.partial(build_body, stage, first, last),
        out_shape=outs,
        in_specs=specs,
        out_specs=out_specs,
        scratch_shapes=scratch,
        input_output_aliases=aliases,
        compiler_params=PARAMS,
        cost_estimate=pl.CostEstimate(
            flops=2 * work, bytes_accessed=len(sources) * 2**24, transcendentals=0
        ),
        name="build",
    )(*operands)


def apply_body(stage, rows, first, last, *refs):
    refs = list(refs)
    number = len(stage)
    mults = refs[:number]
    sources = refs[number : 2 * number]
    del refs[: 2 * number]
    kernels_ref = refs.pop(0)
    if last:
        unary_ref, compat_ref = refs[:2]
        del refs[:2]
    if not first:
        total_in = refs.pop(0)
    out_ref, token_ref = refs[:2]
    del refs[:2]
    probs, tiles, sems, jobs, *rest = refs
    total = rest[0] if last else out_ref
    blocks, classes, pixels = total.shape
    group = blocks * blocks
    pieces = TILES * PARTS
    width = pixels // pieces

    jobs[0, 0] = 0
    for index in range(number):
        for place in range(group):
            count = mults[index][rows[index] * group + place]

            @pl.when(count > 0)
            def _():
                entry = jobs[0, 0] + 1
                jobs[0, 0] = entry
                jobs[entry, 0] = stage[index] * group + place
                jobs[entry, 1] = index * blocks + place // blocks
                jobs[entry, 2] = place % blocks
                jobs[entry, 3] = count

    live = jobs[0, 0]

    def fetch(job, tile):
        hold = lax.rem(job, 2) * pieces + tile
        return pltpu.make_async_copy(
            kernels_ref.at[jobs[job + 1, 0], tile], tiles.at[hold], sems.at[hold]
        )

    for job in range(2):
        @pl.when(job < live)
        def _():
            for tile in range(pieces):
                fetch(job, tile).start()

    token_ref[0] = live
    for block in range(blocks):
        if first:
            total[block] = -sources[0][block].astype(F32)
        else:
            total[block] = total_in[block]
        for index in range(number):
            probs[index * blocks + block] = sources[index][block]

    @pl.loop(0, live)
    def _(job):
        scale = jobs[job + 1, 3].astype(F32)
        index = jobs[job + 1, 1]
        target = jobs[job + 1, 2]
        for tile in range(pieces):
            fetch(job, tile).wait()
            cut = slice(tile * width, (tile + 1) * width)
            total[target, :, cut] += scale * jnp.dot(
                probs[index],
                tiles[lax.rem(job, 2) * pieces + tile],
                preferred_element_type=F32,
            )

            @pl.when(job + 2 < live)
            def _():
                fetch(job + 2, tile).start()

    if last:
        for block in range(blocks):
            out_ref[block] = finish(unary_ref, compat_ref, total[block], block)


def apply(stage, mults, sources, kernels, total, ending):
    blocks, classes, pixels = sources[0].shape
    first, last = total is None, ending is not None
    number = len(sources)
    operands = [*[mult for mult, row in mults], *sources, kernels]
    specs = [SMEM] * number + [VMEM] * number + [ANY]
    if last:
        operands += list(ending)
        specs += [VMEM, VMEM]
    if not first:
        operands.append(total)
        specs.append(VMEM)
    pieces = TILES * PARTS
    outs = [
        jax.ShapeDtypeStruct((blocks, classes, pixels), F32),
        jax.ShapeDtypeStruct((1,), jnp.int32),
    ]
    out_specs = [VMEM, SMEM]
    scratch = [
        pltpu.VMEM((number * blocks, classes, pixels), BF16),
        pltpu.VMEM((2 * pieces, pixels, pixels // pieces), BF16),
        pltpu.SemaphoreType.DMA((2 * pieces,)),
        pltpu.SMEM((number * blocks * blocks + 1, 4), jnp.int32),
    ]
    if last:
        scratch.append(pltpu.VMEM((blocks, classes, pixels), F32))
    return pl.pallas_call(
        functools.partial(apply_body, stage, [row for mult, row in mults], first, last),
        out_shape=outs,
        in_specs=specs,
        out_specs=out_specs,
        scratch_shapes=scratch,
        compiler_params=PARAMS,
        cost_estimate=pl.CostEstimate(
            flops=number * 2 * pixels * pixels * 64, bytes_accessed=number * 2**24, transcendentals=0
        ),
        name="apply",
    )(*operands)


def pick_body(flag_ref, even_ref, odd_ref, after_ref, out_ref):
    @pl.when(flag_ref[0] == 1)
    def _():
        out_ref[...] = even_ref[...]

    @pl.when(flag_ref[0] != 1)
    def _():
        out_ref[...] = odd_ref[...]


def pick(flag, even, odd, after):
    return pl.pallas_call(
        pick_body,
        out_shape=jax.ShapeDtypeStruct(even.shape, even.dtype),
        in_specs=[SMEM, VMEM, VMEM, SMEM],
        out_specs=VMEM,
        compiler_params=SMALL,
        name="pick",
    )(flag, even, odd, after)


def gate_body(value_ref, after_ref, out_ref):
    out_ref[...] = value_ref[...]


def gate(value, after):
    return pl.pallas_call(
        gate_body,
        out_shape=jax.ShapeDtypeStruct(value.shape, value.dtype),
        in_specs=[VMEM, SMEM],
        out_specs=VMEM,
        compiler_params=SMALL,
        name="gate",
    )(value, after)


def permute(value, place):
    count = lax.axis_size("rows")
    moves = [(index, place(index)) for index in range(count)]
    return lax.ppermute(value, "rows", [move for move in moves if 0 <= move[1] < count])


def other_core(value):
    return permute(value, lambda index: index ^ 1)


def even_pair(value):
    return permute(value, lambda index: index ^ 2)


def next_pair(value):
    return permute(value, lambda index: index - 4 if index & 2 else index + 4)


def on_device(unary, features, compat, pairs, pair_count):
    blocks = unary.shape[0]
    me = lax.axis_index("rows")
    core, side = me & 1, (me >> 1) & 1
    off_core = 1 - 2 * core
    off_even = 2 - 4 * side
    offsets = jnp.stack([jnp.zeros_like(off_core), off_core, off_even, -off_even, -off_core])
    info = jnp.concatenate([pairs.reshape(-1), pair_count, offsets.astype(jnp.int32)])
    payload, right = prep(unary, jnp.transpose(features, (1, 0, 2)), info)
    take_even = (core == side).astype(jnp.int32).reshape(1)
    mults = [None] * 5
    kernels = [None]

    def run(value, advance):
        core_value = other_core(value)
        even_value = even_pair(value)
        total, token = advance((0,), [value], None)
        odd_value = next_pair(gate(even_value, token))
        total, token = advance((1, 2), [core_value, even_value], total)
        far_value = other_core(pick(take_even, even_value, odd_value, token))
        total, token = advance((3,), [odd_value], total)
        total, token = advance((4,), [far_value], total)
        return total

    def build_stage(stage, sources, total):
        ending = (unary, compat) if stage[-1] == 4 else None
        total, kernels[0], mult = build(
            stage, info, right, sources, total, kernels[0], 5 * blocks * blocks, ending
        )
        for index, source in enumerate(stage):
            mults[source] = (mult, index)
        return total, mult

    def apply_stage(stage, sources, total):
        ending = (unary, compat) if stage[-1] == 4 else None
        picked = [mults[source] for source in stage]
        return apply(stage, picked, sources, kernels[0], total, ending)

    return run(run(payload, build_stage), apply_stage)


def solution(mesh):
    placed = (
        P(("groups", "rows"), None, None),
        P(("groups", "rows"), None, None),
        P(),
        P(None, ("groups", "rows")),
        P(("groups", "rows")),
    )
    return jax.shard_map(
        on_device,
        mesh=mesh,
        in_specs=placed,
        out_specs=P(("groups", "rows"), None, None),
        check_vma=False,
    )
```

```python
import functools

import jax
import jax.numpy as jnp
from jax import lax
from jax.experimental import pallas as pl
from jax.experimental.pallas import tpu as pltpu
from jax.sharding import PartitionSpec as P

ITERS = 2
FEATS = 5
PART_ROWS = 16
META = 3 * FEATS
DEPTH = 4 * PART_ROWS
ROWS = 256
SPAN = 512
RING = 4
LOG2E = 1.4426950408889634
F32 = jnp.float32
BF16 = jnp.bfloat16
VMEM = pl.BlockSpec(memory_space=pltpu.VMEM)
SMEM = pl.BlockSpec(memory_space=pltpu.SMEM)
ANY = pl.BlockSpec(memory_space=pl.ANY)
PARAMS = pltpu.CompilerParams(vmem_limit_bytes=20 * 2**20)
SMALL = pltpu.CompilerParams(vmem_limit_bytes=16 * 2**20)


def split3(value):
    high = value.astype(BF16)
    rest = value - high.astype(F32)
    middle = rest.astype(BF16)
    low = (rest - middle.astype(F32)).astype(BF16)
    return high, middle, low


def softmax(scores):
    shifted = jnp.exp(scores - jnp.max(scores, axis=0, keepdims=True))
    return shifted / jnp.sum(shifted, axis=0, keepdims=True)


def small_dot(left, right):
    return jnp.dot(left, right, preferred_element_type=F32)


def slot_of(info_ref, slots, slot):
    return [info_ref[part * slots + slot] for part in range(3)]


def slots_of(info_ref):
    return (info_ref.shape[0] - 6) // 3


def is_live(info_ref, slots, slot):
    return slot < info_ref[3 * slots]


def slot_code(info_ref, slots, slot):
    owner, offset, partner = slot_of(info_ref, slots, slot)
    return owner * 6 + offset * 2 + partner


def norm_parts(values):
    norm = jnp.sum(values * values, axis=0, keepdims=True) * (-0.5 * LOG2E)
    return [part.astype(F32) for part in split3(norm)]


def prep_body(unary_ref, feat_ref, info_ref, payload_ref, right_ref):
    blocks, classes, pixels = unary_ref.shape
    slots = slots_of(info_ref)
    row = lax.broadcasted_iota(jnp.int32, (PART_ROWS, 8), 0)
    col = lax.broadcasted_iota(jnp.int32, (PART_ROWS, 8), 1)
    place = [
        jnp.where((row == col + FEATS * part) & (col < FEATS), 1.0, 0.0).astype(BF16)
        for part in range(3)
    ]
    spread = place[0] + place[1] + place[2]
    wide_row = lax.broadcasted_iota(jnp.int32, (PART_ROWS, pixels), 0)
    wide_col = lax.broadcasted_iota(jnp.int32, (PART_ROWS, pixels), 1)
    feat_row = lax.broadcasted_iota(jnp.int32, (8, pixels), 0)
    meta = jnp.zeros((PART_ROWS, pixels), F32)
    for slot in range(slots):
        code = jnp.where(is_live(info_ref, slots, slot), slot_code(info_ref, slots, slot), -1)
        meta = meta + jnp.where((wide_row == META) & (wide_col == code), 1.0, 0.0)
    for block in range(blocks):
        payload_ref[block, :classes, :] = softmax(-unary_ref[block]).astype(BF16)
        values = jnp.zeros((8, pixels), F32)
        for feature in range(FEATS):
            values = jnp.where(feat_row == feature, feat_ref[feature, block : block + 1, :], values)
        parts = split3(values)
        own = meta
        for part in range(3):
            own = own + small_dot(place[part], parts[part])
        payload_ref[block, classes:, :] = own.astype(BF16)
        for index, part in enumerate(split3(values * LOG2E)):
            right_ref[block, index * PART_ROWS : (index + 1) * PART_ROWS, :] = small_dot(
                spread, part
            ).astype(BF16)
        high, middle, low = norm_parts(values)
        norms = jnp.where(wide_row < 3, 1.0, 0.0)
        for index, part in enumerate((high, middle, low)):
            norms = jnp.where(wide_row == 3 + index, part, norms)
        right_ref[block, 3 * PART_ROWS :, :] = norms.astype(BF16)


def prep(unary, feats, info):
    blocks, classes, pixels = unary.shape
    return pl.pallas_call(
        prep_body,
        out_shape=(
            jax.ShapeDtypeStruct((blocks, classes + PART_ROWS, pixels), BF16),
            jax.ShapeDtypeStruct((blocks, DEPTH, pixels), BF16),
        ),
        in_specs=[VMEM, VMEM, SMEM],
        out_specs=(VMEM, VMEM),
        compiler_params=SMALL,
        name="prep",
    )(unary, feats, info)


def left_operand(payload_ref, block, classes):
    pixels = payload_ref.shape[2]
    own = payload_ref[block, classes:, :]
    row = lax.broadcasted_iota(jnp.int32, (8, PART_ROWS), 0)
    col = lax.broadcasted_iota(jnp.int32, (8, PART_ROWS), 1)
    gather = (row < FEATS) & ((col == row) | (col == row + FEATS) | (col == row + 2 * FEATS))
    values = small_dot(jnp.where(gather, 1.0, 0.0).astype(BF16), own)
    wide_row = lax.broadcasted_iota(jnp.int32, (PART_ROWS, pixels), 0)
    norms = jnp.where((wide_row >= 3) & (wide_row < 6), 1.0, 0.0)
    for index, part in enumerate(norm_parts(values)):
        norms = jnp.where(wide_row == index, part, norms)
    return jnp.concatenate([own, own, own, norms.astype(BF16)], axis=0).T


def meta_counts(payload_ref, classes, blocks, offset):
    row = lax.broadcasted_iota(jnp.int32, (PART_ROWS, 128), 0)
    col = lax.broadcasted_iota(jnp.int32, (PART_ROWS, 128), 1)
    own = payload_ref[0, classes:, :128].astype(F32)
    weight = jnp.zeros((PART_ROWS, 128), F32)
    for block in range(blocks):
        for target in range(blocks):
            lane = block * 6 - offset * 2 + target
            step = 8.0 ** (block * blocks + target)
            weight = jnp.where((row == META) & (col == lane), step, weight)
    return jnp.sum(own * weight).astype(jnp.int32)


def finish(unary_ref, compat_ref, message, block):
    scale = 16.0 / unary_ref.shape[2]
    pairwise = jnp.dot(
        compat_ref[...], message, precision=lax.Precision.HIGHEST, preferred_element_type=F32
    )
    return softmax(-unary_ref[block] - pairwise * scale)


def cuts_of(pixels):
    return [slice(start, start + SPAN) for start in range(0, pixels, SPAN)]


def rows_of(chunk):
    return slice(chunk * ROWS, (chunk + 1) * ROWS)


def local_count(info_ref, slots):
    count = jnp.int32(0)
    for slot in range(slots):
        hit = is_live(info_ref, slots, slot) & (slot_of(info_ref, slots, slot)[1] == 0)
        count = count + jnp.where(hit, 1, 0)
    return count


def own_body(info_ref, right_ref, payload_ref, probs_ref, total_ref, token_ref, left, *sets):
    blocks, classes, pixels = total_ref.shape
    slots = slots_of(info_ref)
    count = local_count(info_ref, slots)
    token_ref[0] = count
    for block in range(blocks):
        total_ref[block] = -probs_ref[block, :classes, :].astype(F32)
        left[block] = left_operand(payload_ref, block, classes)

    def product(block, target, chunk, hold, cut, scale):
        part = jnp.dot(
            probs_ref[block, :classes, rows_of(chunk)], sets[hold][:, cut], preferred_element_type=F32
        )
        total_ref[target, :, cut] += part if scale is None else scale * part

    def run(jobs, scale):
        steps = [(block, target, chunk) for block, target in jobs for chunk in range(pixels // ROWS)]
        earlier = None
        for number, (block, target, chunk) in enumerate(steps):
            hold = number % len(sets)
            for cut in cuts_of(pixels):
                scores = jnp.dot(
                    left[block, rows_of(chunk), :], right_ref[target, :, cut], preferred_element_type=F32
                )
                sets[hold][:, cut] = jnp.exp2(scores).astype(BF16)
                if earlier is not None:
                    product(*earlier, cut, scale)
            earlier = block, target, chunk, hold
        for cut in cuts_of(pixels):
            product(*earlier, cut, scale)

    run([(block, block) for block in range(blocks)], None)

    @pl.when(count > 0)
    def _():
        pairs = [(block, target) for block in range(blocks) for target in range(blocks)]
        run([pair for pair in pairs if pair[0] != pair[1]], count.astype(F32))


def own(info, right, payload, probs):
    blocks, rows, pixels = payload.shape
    classes = rows - PART_ROWS
    return pl.pallas_call(
        own_body,
        out_shape=(
            jax.ShapeDtypeStruct((blocks, classes, pixels), F32),
            jax.ShapeDtypeStruct((1,), jnp.int32),
        ),
        in_specs=[SMEM, VMEM, VMEM, VMEM],
        out_specs=(VMEM, SMEM),
        scratch_shapes=[
            pltpu.VMEM((blocks, pixels, DEPTH), BF16),
            *[pltpu.VMEM((ROWS, pixels), BF16) for ring in range(RING)],
        ],
        compiler_params=PARAMS,
        cost_estimate=pl.CostEstimate(
            flops=2 * 4 * pixels * pixels * 640, bytes_accessed=2**22, transcendentals=0
        ),
        name="own",
    )(info, right, payload, probs)


def remote_body(stage, ending, *refs):
    refs = list(refs)
    info_ref, right_ref = refs[:2]
    payloads = refs[2 : 2 + len(stage)]
    sources = refs[2 + len(stage) : 2 + 2 * len(stage)]
    del refs[: 2 + 2 * len(stage)]
    if ending:
        unary_ref, compat_ref = refs[:2]
        del refs[:2]
    total_in, total_ref, token_ref, left, probs, jobs, *bufs = refs
    total = bufs.pop() if ending else total_ref
    blocks, classes, pixels = total.shape
    slots = slots_of(info_ref)
    chunks = pixels // ROWS

    for column in range(4):
        jobs[0, column] = 0
    bufs[-1][...] = jnp.zeros_like(bufs[-1])
    for block in range(blocks):
        total[block] = total_in[block]

    for index, (source, payload_ref) in enumerate(zip(stage, payloads)):
        offset = info_ref[3 * slots + 1 + source]
        packed = meta_counts(payload_ref, classes, blocks, offset)

        def multiplicity(block, target):
            ahead = jnp.int32(0)
            for slot in range(slots):
                owner, distance, partner = slot_of(info_ref, slots, slot)
                hit = (owner == target) & (distance == offset) & (partner == block)
                ahead = ahead + jnp.where(hit & is_live(info_ref, slots, slot), 1, 0)
            behind = lax.shift_right_logical(packed, 3 * (block * blocks + target)) & 7
            return jnp.where(offset > 0, ahead, behind)

        @pl.loop(0, blocks)
        def _(block):
            counts = [multiplicity(block, target) for target in range(blocks)]
            for target in range(blocks):
                @pl.when(counts[target] > 0)
                def _():
                    entry = jobs[0, 0] + 1
                    jobs[0, 0] = entry
                    jobs[entry, 1] = index * blocks + block
                    jobs[entry, 2] = target
                    jobs[entry, 3] = counts[target]

            @pl.when(sum(counts) > 0)
            def _():
                left[index * blocks + block] = left_operand(payload_ref, block, classes)
                probs[index * blocks + block] = sources[index][block, :classes, :]

    number = jobs[0, 0]
    token_ref[0] = number

    def product(entry, chunk, cut):
        index, target, count = entry
        share = jnp.dot(
            probs[index, :, rows_of(chunk)],
            bufs[chunk % RING][:, cut],
            preferred_element_type=F32,
        )
        total[target, :, cut] += count.astype(F32) * share

    @pl.loop(0, number)
    def _(job):
        entry = index, target, count = [jobs[job + 1, column] for column in range(1, 4)]
        earlier = [jobs[job, column] for column in range(1, 4)]
        for chunk in range(chunks):
            for cut in cuts_of(pixels):
                scores = jnp.dot(
                    left[index, rows_of(chunk), :], right_ref[target, :, cut], preferred_element_type=F32
                )
                bufs[chunk % RING][:, cut] = jnp.exp2(scores).astype(BF16)
                if chunk > 0:
                    product(entry, chunk - 1, cut)
                else:
                    product(earlier, chunks - 1, cut)

    @pl.when(number > 0)
    def _():
        entry = [jobs[number, column] for column in range(1, 4)]
        for cut in cuts_of(pixels):
            product(entry, chunks - 1, cut)

    if ending:
        for block in range(blocks):
            result = finish(unary_ref, compat_ref, total[block], block)
            total_ref[block] = result.astype(total_ref.dtype)


def remote(stage, info, right, payloads, sources, total, ending, out_type):
    blocks, classes, pixels = total.shape
    number = len(stage)
    operands = [info, right, *payloads, *sources, *ending, total]
    specs = [SMEM] + [VMEM] * (len(operands) - 1)
    scratch = [
        pltpu.VMEM((number * blocks, pixels, DEPTH), BF16),
        pltpu.VMEM((number * blocks, classes, pixels), BF16),
        pltpu.SMEM((number * blocks * blocks + 1, 4), jnp.int32),
        *[pltpu.VMEM((ROWS, pixels), BF16) for ring in range(RING)],
    ]
    if ending:
        scratch.append(pltpu.VMEM((blocks, classes, pixels), F32))
    return pl.pallas_call(
        functools.partial(remote_body, stage, bool(ending)),
        out_shape=(
            jax.ShapeDtypeStruct((blocks, classes, pixels), out_type),
            jax.ShapeDtypeStruct((1,), jnp.int32),
        ),
        in_specs=specs,
        out_specs=(VMEM, SMEM),
        scratch_shapes=scratch,
        compiler_params=PARAMS,
        cost_estimate=pl.CostEstimate(
            flops=2 * number * 2 * pixels * pixels * 640, bytes_accessed=2**22, transcendentals=0
        ),
        name="remote",
    )(*operands)


def pick_body(flag_ref, even_ref, odd_ref, after_ref, out_ref):
    @pl.when(flag_ref[0] == 1)
    def _():
        out_ref[...] = even_ref[...]

    @pl.when(flag_ref[0] != 1)
    def _():
        out_ref[...] = odd_ref[...]


def pick(flag, even, odd, after):
    return pl.pallas_call(
        pick_body,
        out_shape=jax.ShapeDtypeStruct(even.shape, even.dtype),
        in_specs=[SMEM, VMEM, VMEM, SMEM],
        out_specs=VMEM,
        compiler_params=SMALL,
        name="pick",
    )(flag, even, odd, after)


def gate_body(value_ref, after_ref, out_ref):
    out_ref[...] = value_ref[...]


def gate(value, after):
    return pl.pallas_call(
        gate_body,
        out_shape=jax.ShapeDtypeStruct(value.shape, value.dtype),
        in_specs=[VMEM, SMEM],
        out_specs=VMEM,
        compiler_params=SMALL,
        name="gate",
    )(value, after)


def permute(value, place):
    count = lax.axis_size("rows")
    moves = [(index, place(index)) for index in range(count)]
    return lax.ppermute(value, "rows", [move for move in moves if 0 <= move[1] < count])


def other_core(value):
    return permute(value, lambda index: index ^ 1)


def even_pair(value):
    return permute(value, lambda index: index ^ 2)


def next_pair(value):
    return permute(value, lambda index: index - 4 if index & 2 else index + 4)


def on_device(unary, features, compat, pairs, pair_count):
    blocks = unary.shape[0]
    me = lax.axis_index("rows")
    core, side = me & 1, (me >> 1) & 1
    off_core = 1 - 2 * core
    off_even = 2 - 4 * side
    offsets = jnp.stack([jnp.zeros_like(off_core), off_core, off_even, -off_even, -off_core])
    info = jnp.concatenate([pairs.reshape(-1), pair_count, offsets.astype(jnp.int32)])
    payload, right = prep(unary, jnp.transpose(features, (1, 0, 2)), info)
    take_even = (core == side).astype(jnp.int32).reshape(1)
    payloads = [payload]

    def run(value, out_type):
        core_value = other_core(value)
        even_value = even_pair(value)
        window = [value, core_value, even_value]
        total, token = own(info, right, payload, value)

        def advance(stage, total, ending=()):
            taken = [[values[source] for source in stage] for values in (payloads, window)]
            kind = out_type if ending else F32
            return remote(stage, info, right, *taken, total, ending, kind)

        window.append(next_pair(gate(even_value, token)))
        if len(payloads) == 1:
            payloads.extend(window[1:])
        total, token = advance((1, 2), total)
        window.append(other_core(pick(take_even, even_value, window[3], token)))
        if len(payloads) == 4:
            payloads.append(window[4])
        total, token = advance((3,), total)
        total, token = advance((4,), total, (unary, compat))
        return total

    return run(run(payload, BF16), F32)


def solution(mesh):
    placed = (
        P(("groups", "rows"), None, None),
        P(("groups", "rows"), None, None),
        P(),
        P(None, ("groups", "rows")),
        P(("groups", "rows")),
    )
    return jax.shard_map(
        on_device,
        mesh=mesh,
        in_specs=placed,
        out_specs=P(("groups", "rows"), None, None),
        check_vma=False,
    )
```

```python
import functools

import jax
import jax.numpy as jnp
from jax import lax
from jax.experimental import pallas as pl
from jax.experimental.pallas import tpu as pltpu
from jax.sharding import PartitionSpec as P

ITERS = 2
FEATS = 5
PART_ROWS = 16
META = 3 * FEATS
DEPTH = 4 * PART_ROWS
ROWS = 256
SPAN = 512
RING = 4
LOG2E = 1.4426950408889634
F32 = jnp.float32
BF16 = jnp.bfloat16
VMEM = pl.BlockSpec(memory_space=pltpu.VMEM)
SMEM = pl.BlockSpec(memory_space=pltpu.SMEM)
ANY = pl.BlockSpec(memory_space=pl.ANY)
PARAMS = pltpu.CompilerParams(vmem_limit_bytes=20 * 2**20)
SMALL = pltpu.CompilerParams(vmem_limit_bytes=16 * 2**20)


def split3(value):
    high = value.astype(BF16)
    rest = value - high.astype(F32)
    middle = rest.astype(BF16)
    low = (rest - middle.astype(F32)).astype(BF16)
    return high, middle, low


def softmax(scores):
    shifted = jnp.exp(scores - jnp.max(scores, axis=0, keepdims=True))
    return shifted / jnp.sum(shifted, axis=0, keepdims=True)


def small_dot(left, right):
    return jnp.dot(left, right, preferred_element_type=F32)


def slot_of(info_ref, slots, slot):
    return [info_ref[part * slots + slot] for part in range(3)]


def slots_of(info_ref):
    return (info_ref.shape[0] - 6) // 3


def is_live(info_ref, slots, slot):
    return slot < info_ref[3 * slots]


def slot_code(info_ref, slots, slot):
    owner, offset, partner = slot_of(info_ref, slots, slot)
    return owner * 6 + offset * 2 + partner


def norm_parts(values):
    norm = jnp.sum(values * values, axis=0, keepdims=True) * (-0.5 * LOG2E)
    return [part.astype(F32) for part in split3(norm)]


def prep_body(unary_ref, feat_ref, info_ref, payload_ref, right_ref):
    blocks, classes, pixels = unary_ref.shape
    slots = slots_of(info_ref)
    row = lax.broadcasted_iota(jnp.int32, (PART_ROWS, 8), 0)
    col = lax.broadcasted_iota(jnp.int32, (PART_ROWS, 8), 1)
    place = [
        jnp.where((row == col + FEATS * part) & (col < FEATS), 1.0, 0.0).astype(BF16)
        for part in range(3)
    ]
    spread = place[0] + place[1] + place[2]
    wide_row = lax.broadcasted_iota(jnp.int32, (PART_ROWS, pixels), 0)
    wide_col = lax.broadcasted_iota(jnp.int32, (PART_ROWS, pixels), 1)
    feat_row = lax.broadcasted_iota(jnp.int32, (8, pixels), 0)
    meta = jnp.zeros((PART_ROWS, pixels), F32)
    for slot in range(slots):
        code = jnp.where(is_live(info_ref, slots, slot), slot_code(info_ref, slots, slot), -1)
        meta = meta + jnp.where((wide_row == META) & (wide_col == code), 1.0, 0.0)
    for block in range(blocks):
        payload_ref[block, :classes, :] = softmax(-unary_ref[block]).astype(BF16)
        values = jnp.zeros((8, pixels), F32)
        for feature in range(FEATS):
            values = jnp.where(feat_row == feature, feat_ref[feature, block : block + 1, :], values)
        parts = split3(values)
        own = meta
        for part in range(3):
            own = own + small_dot(place[part], parts[part])
        payload_ref[block, classes:, :] = own.astype(BF16)
        for index, part in enumerate(split3(values * LOG2E)):
            right_ref[block, index * PART_ROWS : (index + 1) * PART_ROWS, :] = small_dot(
                spread, part
            ).astype(BF16)
        high, middle, low = norm_parts(values)
        norms = jnp.where(wide_row < 3, 1.0, 0.0)
        for index, part in enumerate((high, middle, low)):
            norms = jnp.where(wide_row == 3 + index, part, norms)
        right_ref[block, 3 * PART_ROWS :, :] = norms.astype(BF16)


def prep(unary, feats, info):
    blocks, classes, pixels = unary.shape
    return pl.pallas_call(
        prep_body,
        out_shape=(
            jax.ShapeDtypeStruct((blocks, classes + PART_ROWS, pixels), BF16),
            jax.ShapeDtypeStruct((blocks, DEPTH, pixels), BF16),
        ),
        in_specs=[VMEM, VMEM, SMEM],
        out_specs=(VMEM, VMEM),
        compiler_params=SMALL,
        name="prep",
    )(unary, feats, info)


def left_operand(payload_ref, block, classes):
    pixels = payload_ref.shape[2]
    own = payload_ref[block, classes:, :]
    row = lax.broadcasted_iota(jnp.int32, (8, PART_ROWS), 0)
    col = lax.broadcasted_iota(jnp.int32, (8, PART_ROWS), 1)
    gather = (row < FEATS) & ((col == row) | (col == row + FEATS) | (col == row + 2 * FEATS))
    values = small_dot(jnp.where(gather, 1.0, 0.0).astype(BF16), own)
    wide_row = lax.broadcasted_iota(jnp.int32, (PART_ROWS, pixels), 0)
    norms = jnp.where((wide_row >= 3) & (wide_row < 6), 1.0, 0.0)
    for index, part in enumerate(norm_parts(values)):
        norms = jnp.where(wide_row == index, part, norms)
    return jnp.concatenate([own, own, own, norms.astype(BF16)], axis=0).T


def meta_counts(payload_ref, classes, blocks, offset):
    row = lax.broadcasted_iota(jnp.int32, (PART_ROWS, 128), 0)
    col = lax.broadcasted_iota(jnp.int32, (PART_ROWS, 128), 1)
    own = payload_ref[0, classes:, :128].astype(F32)
    weight = jnp.zeros((PART_ROWS, 128), F32)
    for block in range(blocks):
        for target in range(blocks):
            lane = block * 6 - offset * 2 + target
            step = 8.0 ** (block * blocks + target)
            weight = jnp.where((row == META) & (col == lane), step, weight)
    return jnp.sum(own * weight).astype(jnp.int32)


def finish(unary_ref, compat_ref, message, block):
    scale = 16.0 / unary_ref.shape[2]
    pairwise = jnp.dot(
        compat_ref[...], message, precision=lax.Precision.HIGHEST, preferred_element_type=F32
    )
    return softmax(-unary_ref[block] - pairwise * scale)


def cuts_of(pixels):
    return [slice(start, start + SPAN) for start in range(0, pixels, SPAN)]


def rows_of(chunk):
    return slice(chunk * ROWS, (chunk + 1) * ROWS)


def local_count(info_ref, slots):
    count = jnp.int32(0)
    for slot in range(slots):
        hit = is_live(info_ref, slots, slot) & (slot_of(info_ref, slots, slot)[1] == 0)
        count = count + jnp.where(hit, 1, 0)
    return count


def sweep(jobs, left, right_ref, probs, bufs, total):
    pixels = right_ref.shape[2]
    chunks = pixels // ROWS
    number = jobs[0, 0]

    def product(entry, chunk, cut):
        index, target, count = entry
        share = jnp.dot(
            probs[index, :, rows_of(chunk)],
            bufs[chunk % RING][:, cut],
            preferred_element_type=F32,
        )
        total[target, :, cut] += count.astype(F32) * share

    @pl.loop(0, number)
    def _(job):
        entry = index, target, count = [jobs[job + 1, column] for column in range(1, 4)]
        earlier = [jobs[job, column] for column in range(1, 4)]
        for chunk in range(chunks):
            for cut in cuts_of(pixels):
                scores = jnp.dot(
                    left[index, rows_of(chunk), :], right_ref[target, :, cut], preferred_element_type=F32
                )
                bufs[chunk % RING][:, cut] = jnp.exp2(scores).astype(BF16)
                if chunk > 0:
                    product(entry, chunk - 1, cut)
                else:
                    product(earlier, chunks - 1, cut)

    @pl.when(number > 0)
    def _():
        entry = [jobs[number, column] for column in range(1, 4)]
        for cut in cuts_of(pixels):
            product(entry, chunks - 1, cut)


def clear(jobs, bufs):
    for column in range(4):
        jobs[0, column] = 0
    bufs[-1][...] = jnp.zeros_like(bufs[-1])


def own_body(info_ref, right_ref, payload_ref, probs_ref, total_ref, token_ref, left, probs, jobs, *bufs):
    blocks, classes, pixels = total_ref.shape
    slots = slots_of(info_ref)
    count = local_count(info_ref, slots)
    token_ref[0] = count
    clear(jobs, bufs)
    for block in range(blocks):
        total_ref[block] = -probs_ref[block, :classes, :].astype(F32)
        probs[block] = probs_ref[block, :classes, :]
        left[block] = left_operand(payload_ref, block, classes)
    pairs = [(block, target) for block in range(blocks) for target in range(blocks)]
    for number, (block, target) in enumerate(sorted(pairs, key=lambda pair: pair[0] != pair[1])):
        jobs[number + 1, 1] = block
        jobs[number + 1, 2] = target
        jobs[number + 1, 3] = 1 if block == target else count
    jobs[0, 0] = jnp.where(count > 0, blocks * blocks, blocks)
    sweep(jobs, left, right_ref, probs, bufs, total_ref)


def own(info, right, payload, probs):
    blocks, rows, pixels = payload.shape
    classes = rows - PART_ROWS
    return pl.pallas_call(
        own_body,
        out_shape=(
            jax.ShapeDtypeStruct((blocks, classes, pixels), F32),
            jax.ShapeDtypeStruct((1,), jnp.int32),
        ),
        in_specs=[SMEM, VMEM, VMEM, VMEM],
        out_specs=(VMEM, SMEM),
        scratch_shapes=[
            pltpu.VMEM((blocks, pixels, DEPTH), BF16),
            pltpu.VMEM((blocks, classes, pixels), BF16),
            pltpu.SMEM((blocks * blocks + 1, 4), jnp.int32),
            *[pltpu.VMEM((ROWS, pixels), BF16) for ring in range(RING)],
        ],
        compiler_params=PARAMS,
        cost_estimate=pl.CostEstimate(
            flops=2 * 4 * pixels * pixels * 640, bytes_accessed=2**22, transcendentals=0
        ),
        name="own",
    )(info, right, payload, probs)


def remote_body(stage, ending, *refs):
    refs = list(refs)
    info_ref, right_ref = refs[:2]
    payloads = refs[2 : 2 + len(stage)]
    sources = refs[2 + len(stage) : 2 + 2 * len(stage)]
    del refs[: 2 + 2 * len(stage)]
    if ending:
        unary_ref, compat_ref = refs[:2]
        del refs[:2]
    total_in, total_ref, token_ref, left, probs, jobs, *bufs = refs
    total = bufs.pop() if ending else total_ref
    blocks, classes, pixels = total.shape
    slots = slots_of(info_ref)

    clear(jobs, bufs)
    for block in range(blocks):
        total[block] = total_in[block]

    for index, (source, payload_ref) in enumerate(zip(stage, payloads)):
        offset = info_ref[3 * slots + 1 + source]
        packed = meta_counts(payload_ref, classes, blocks, offset)

        def multiplicity(block, target):
            ahead = jnp.int32(0)
            for slot in range(slots):
                owner, distance, partner = slot_of(info_ref, slots, slot)
                hit = (owner == target) & (distance == offset) & (partner == block)
                ahead = ahead + jnp.where(hit & is_live(info_ref, slots, slot), 1, 0)
            behind = lax.shift_right_logical(packed, 3 * (block * blocks + target)) & 7
            return jnp.where(offset > 0, ahead, behind)

        @pl.loop(0, blocks)
        def _(block):
            counts = [multiplicity(block, target) for target in range(blocks)]
            for target in range(blocks):
                @pl.when(counts[target] > 0)
                def _():
                    entry = jobs[0, 0] + 1
                    jobs[0, 0] = entry
                    jobs[entry, 1] = index * blocks + block
                    jobs[entry, 2] = target
                    jobs[entry, 3] = counts[target]

            @pl.when(sum(counts) > 0)
            def _():
                left[index * blocks + block] = left_operand(payload_ref, block, classes)
                probs[index * blocks + block] = sources[index][block, :classes, :]

    token_ref[0] = jobs[0, 0]
    sweep(jobs, left, right_ref, probs, bufs, total)

    if ending:
        for block in range(blocks):
            result = finish(unary_ref, compat_ref, total[block], block)
            total_ref[block] = result.astype(total_ref.dtype)


def remote(stage, info, right, payloads, sources, total, ending, out_type):
    blocks, classes, pixels = total.shape
    number = len(stage)
    operands = [info, right, *payloads, *sources, *ending, total]
    specs = [SMEM] + [VMEM] * (len(operands) - 1)
    scratch = [
        pltpu.VMEM((number * blocks, pixels, DEPTH), BF16),
        pltpu.VMEM((number * blocks, classes, pixels), BF16),
        pltpu.SMEM((number * blocks * blocks + 1, 4), jnp.int32),
        *[pltpu.VMEM((ROWS, pixels), BF16) for ring in range(RING)],
    ]
    if ending:
        scratch.append(pltpu.VMEM((blocks, classes, pixels), F32))
    return pl.pallas_call(
        functools.partial(remote_body, stage, bool(ending)),
        out_shape=(
            jax.ShapeDtypeStruct((blocks, classes, pixels), out_type),
            jax.ShapeDtypeStruct((1,), jnp.int32),
        ),
        in_specs=specs,
        out_specs=(VMEM, SMEM),
        scratch_shapes=scratch,
        compiler_params=PARAMS,
        cost_estimate=pl.CostEstimate(
            flops=2 * number * 2 * pixels * pixels * 640, bytes_accessed=2**22, transcendentals=0
        ),
        name="remote",
    )(*operands)


def pick_body(flag_ref, even_ref, odd_ref, after_ref, out_ref):
    @pl.when(flag_ref[0] == 1)
    def _():
        out_ref[...] = even_ref[...]

    @pl.when(flag_ref[0] != 1)
    def _():
        out_ref[...] = odd_ref[...]


def pick(flag, even, odd, after):
    return pl.pallas_call(
        pick_body,
        out_shape=jax.ShapeDtypeStruct(even.shape, even.dtype),
        in_specs=[SMEM, VMEM, VMEM, SMEM],
        out_specs=VMEM,
        compiler_params=SMALL,
        name="pick",
    )(flag, even, odd, after)


def gate_body(value_ref, after_ref, out_ref):
    out_ref[...] = value_ref[...]


def gate(value, after):
    return pl.pallas_call(
        gate_body,
        out_shape=jax.ShapeDtypeStruct(value.shape, value.dtype),
        in_specs=[VMEM, SMEM],
        out_specs=VMEM,
        compiler_params=SMALL,
        name="gate",
    )(value, after)


def permute(value, place):
    count = lax.axis_size("rows")
    moves = [(index, place(index)) for index in range(count)]
    return lax.ppermute(value, "rows", [move for move in moves if 0 <= move[1] < count])


def other_core(value):
    return permute(value, lambda index: index ^ 1)


def even_pair(value):
    return permute(value, lambda index: index ^ 2)


def next_pair(value):
    return permute(value, lambda index: index - 4 if index & 2 else index + 4)


def on_device(unary, features, compat, pairs, pair_count):
    blocks = unary.shape[0]
    me = lax.axis_index("rows")
    core, side = me & 1, (me >> 1) & 1
    off_core = 1 - 2 * core
    off_even = 2 - 4 * side
    offsets = jnp.stack([jnp.zeros_like(off_core), off_core, off_even, -off_even, -off_core])
    info = jnp.concatenate([pairs.reshape(-1), pair_count, offsets.astype(jnp.int32)])
    payload, right = prep(unary, jnp.transpose(features, (1, 0, 2)), info)
    take_even = (core == side).astype(jnp.int32).reshape(1)
    payloads = [payload]

    def run(value, out_type):
        core_value = other_core(value)
        even_value = even_pair(value)
        window = [value, core_value, even_value]
        total, token = own(info, right, payload, value)

        def advance(stage, total, ending=()):
            taken = [[values[source] for source in stage] for values in (payloads, window)]
            kind = out_type if ending else F32
            return remote(stage, info, right, *taken, total, ending, kind)

        window.append(next_pair(gate(even_value, token)))
        if len(payloads) == 1:
            payloads.extend(window[1:])
        total, token = advance((1, 2), total)
        window.append(other_core(pick(take_even, even_value, window[3], token)))
        if len(payloads) == 4:
            payloads.append(window[4])
        total, token = advance((3,), total)
        total, token = advance((4,), total, (unary, compat))
        return total

    return run(run(payload, BF16), F32)


def solution(mesh):
    placed = (
        P(("groups", "rows"), None, None),
        P(("groups", "rows"), None, None),
        P(),
        P(None, ("groups", "rows")),
        P(("groups", "rows")),
    )
    return jax.shard_map(
        on_device,
        mesh=mesh,
        in_specs=placed,
        out_specs=P(("groups", "rows"), None, None),
        check_vma=False,
    )
```

```python
import functools

import jax
import jax.numpy as jnp
from jax import lax
from jax.experimental import pallas as pl
from jax.experimental.pallas import tpu as pltpu
from jax.sharding import PartitionSpec as P

ITERS = 2
FEATS = 5
PART_ROWS = 16
META = 3 * FEATS
DEPTH = 4 * PART_ROWS
ROWS = 256
SPAN = 512
RING = 4
LOG2E = 1.4426950408889634
F32 = jnp.float32
BF16 = jnp.bfloat16
VMEM = pl.BlockSpec(memory_space=pltpu.VMEM)
SMEM = pl.BlockSpec(memory_space=pltpu.SMEM)
ANY = pl.BlockSpec(memory_space=pl.ANY)
PARAMS = pltpu.CompilerParams(vmem_limit_bytes=20 * 2**20)
SMALL = pltpu.CompilerParams(vmem_limit_bytes=16 * 2**20)


def split3(value):
    high = value.astype(BF16)
    rest = value - high.astype(F32)
    middle = rest.astype(BF16)
    low = (rest - middle.astype(F32)).astype(BF16)
    return high, middle, low


def softmax(scores):
    shifted = jnp.exp(scores - jnp.max(scores, axis=0, keepdims=True))
    return shifted / jnp.sum(shifted, axis=0, keepdims=True)


def small_dot(left, right):
    return jnp.dot(left, right, preferred_element_type=F32)


def slot_of(info_ref, slots, slot):
    return [info_ref[part * slots + slot] for part in range(3)]


def slots_of(info_ref):
    return (info_ref.shape[0] - 6) // 3


def is_live(info_ref, slots, slot):
    return slot < info_ref[3 * slots]


def slot_code(info_ref, slots, slot):
    owner, offset, partner = slot_of(info_ref, slots, slot)
    return owner * 6 + offset * 2 + partner


def norm_parts(values):
    norm = jnp.sum(values * values, axis=0, keepdims=True) * (-0.5 * LOG2E)
    return [part.astype(F32) for part in split3(norm)]


def prep_body(unary_ref, feat_ref, info_ref, payload_ref, right_ref):
    blocks, classes, pixels = unary_ref.shape
    slots = slots_of(info_ref)
    row = lax.broadcasted_iota(jnp.int32, (PART_ROWS, 8), 0)
    col = lax.broadcasted_iota(jnp.int32, (PART_ROWS, 8), 1)
    place = [
        jnp.where((row == col + FEATS * part) & (col < FEATS), 1.0, 0.0).astype(BF16)
        for part in range(3)
    ]
    spread = place[0] + place[1] + place[2]
    wide_row = lax.broadcasted_iota(jnp.int32, (PART_ROWS, pixels), 0)
    wide_col = lax.broadcasted_iota(jnp.int32, (PART_ROWS, pixels), 1)
    feat_row = lax.broadcasted_iota(jnp.int32, (8, pixels), 0)
    meta = jnp.zeros((PART_ROWS, pixels), F32)
    for slot in range(slots):
        code = jnp.where(is_live(info_ref, slots, slot), slot_code(info_ref, slots, slot), -1)
        meta = meta + jnp.where((wide_row == META) & (wide_col == code), 1.0, 0.0)
    for block in range(blocks):
        payload_ref[block, :classes, :] = softmax(-unary_ref[block]).astype(BF16)
        values = jnp.zeros((8, pixels), F32)
        for feature in range(FEATS):
            values = jnp.where(feat_row == feature, feat_ref[feature, block : block + 1, :], values)
        parts = split3(values)
        own = meta
        for part in range(3):
            own = own + small_dot(place[part], parts[part])
        payload_ref[block, classes:, :] = own.astype(BF16)
        for index, part in enumerate(split3(values * LOG2E)):
            right_ref[block, index * PART_ROWS : (index + 1) * PART_ROWS, :] = small_dot(
                spread, part
            ).astype(BF16)
        high, middle, low = norm_parts(values)
        norms = jnp.where(wide_row < 3, 1.0, 0.0)
        for index, part in enumerate((high, middle, low)):
            norms = jnp.where(wide_row == 3 + index, part, norms)
        right_ref[block, 3 * PART_ROWS :, :] = norms.astype(BF16)


def prep(unary, feats, info):
    blocks, classes, pixels = unary.shape
    return pl.pallas_call(
        prep_body,
        out_shape=(
            jax.ShapeDtypeStruct((blocks, classes + PART_ROWS, pixels), BF16),
            jax.ShapeDtypeStruct((blocks, DEPTH, pixels), BF16),
        ),
        in_specs=[VMEM, VMEM, SMEM],
        out_specs=(VMEM, VMEM),
        compiler_params=SMALL,
        name="prep",
    )(unary, feats, info)


def left_operand(payload_ref, block, classes):
    pixels = payload_ref.shape[2]
    own = payload_ref[block, classes:, :]
    row = lax.broadcasted_iota(jnp.int32, (8, PART_ROWS), 0)
    col = lax.broadcasted_iota(jnp.int32, (8, PART_ROWS), 1)
    gather = (row < FEATS) & ((col == row) | (col == row + FEATS) | (col == row + 2 * FEATS))
    values = small_dot(jnp.where(gather, 1.0, 0.0).astype(BF16), own)
    wide_row = lax.broadcasted_iota(jnp.int32, (PART_ROWS, pixels), 0)
    norms = jnp.where((wide_row >= 3) & (wide_row < 6), 1.0, 0.0)
    for index, part in enumerate(norm_parts(values)):
        norms = jnp.where(wide_row == index, part, norms)
    return jnp.concatenate([own, own, own, norms.astype(BF16)], axis=0).T


def meta_counts(payload_ref, classes, blocks, offset):
    row = lax.broadcasted_iota(jnp.int32, (PART_ROWS, 128), 0)
    col = lax.broadcasted_iota(jnp.int32, (PART_ROWS, 128), 1)
    own = payload_ref[0, classes:, :128].astype(F32)
    weight = jnp.zeros((PART_ROWS, 128), F32)
    for block in range(blocks):
        for target in range(blocks):
            lane = block * 6 - offset * 2 + target
            step = 8.0 ** (block * blocks + target)
            weight = jnp.where((row == META) & (col == lane), step, weight)
    return jnp.sum(own * weight).astype(jnp.int32)


def finish(unary_ref, compat_ref, message, block):
    scale = 16.0 / unary_ref.shape[2]
    pairwise = jnp.dot(
        compat_ref[...], message, precision=lax.Precision.HIGHEST, preferred_element_type=F32
    )
    return softmax(-unary_ref[block] - pairwise * scale)


def cuts_of(pixels):
    return [slice(start, start + SPAN) for start in range(0, pixels, SPAN)]


def rows_of(chunk):
    return slice(chunk * ROWS, (chunk + 1) * ROWS)


def local_count(info_ref, slots):
    count = jnp.int32(0)
    for slot in range(slots):
        hit = is_live(info_ref, slots, slot) & (slot_of(info_ref, slots, slot)[1] == 0)
        count = count + jnp.where(hit, 1, 0)
    return count


def sweep(jobs, left, right_ref, probs, bufs, total):
    pixels = right_ref.shape[2]
    chunks = pixels // ROWS
    number = jobs[0, 0]

    def product(entry, chunk, cut):
        index, target, count = entry
        share = jnp.dot(
            probs[index, :, rows_of(chunk)],
            bufs[chunk % RING][:, cut],
            preferred_element_type=F32,
        )
        total[target, :, cut] += count.astype(F32) * share

    @pl.loop(0, number)
    def _(job):
        entry = index, target, count = [jobs[job + 1, column] for column in range(1, 4)]
        earlier = [jobs[job, column] for column in range(1, 4)]
        for chunk in range(chunks):
            for cut in cuts_of(pixels):
                scores = jnp.dot(
                    left[index, rows_of(chunk), :], right_ref[target, :, cut], preferred_element_type=F32
                )
                bufs[chunk % RING][:, cut] = jnp.exp2(scores).astype(BF16)
                if chunk > 0:
                    product(entry, chunk - 1, cut)
                else:
                    product(earlier, chunks - 1, cut)

    @pl.when(number > 0)
    def _():
        entry = [jobs[number, column] for column in range(1, 4)]
        for cut in cuts_of(pixels):
            product(entry, chunks - 1, cut)


def clear(jobs, bufs):
    for column in range(4):
        jobs[0, column] = 0
    bufs[-1][...] = jnp.zeros_like(bufs[-1])


def own_body(info_ref, right_ref, payload_ref, total_ref, token_ref, left, jobs, probs, *bufs):
    blocks, classes, pixels = total_ref.shape
    slots = slots_of(info_ref)
    count = local_count(info_ref, slots)
    token_ref[0] = count
    clear(jobs, bufs)
    for block in range(blocks):
        total_ref[block] = -payload_ref[block, :classes, :].astype(F32)
        probs[block] = payload_ref[block, :classes, :]
        left[block] = left_operand(payload_ref, block, classes)
    pairs = [(block, target) for block in range(blocks) for target in range(blocks)]
    for number, (block, target) in enumerate(sorted(pairs, key=lambda pair: pair[0] != pair[1])):
        jobs[number + 1, 1] = block
        jobs[number + 1, 2] = target
        jobs[number + 1, 3] = 1 if block == target else count
    jobs[0, 0] = jnp.where(count > 0, blocks * blocks, blocks)
    sweep(jobs, left, right_ref, probs, bufs, total_ref)


def buffers(pixels):
    return [pltpu.VMEM((ROWS, pixels), BF16) for ring in range(RING)]


def stage_cost(sources, pixels):
    return pl.CostEstimate(
        flops=2 * 2 * sources * pixels * pixels * 640, bytes_accessed=2**22, transcendentals=0
    )


def plan_shapes(sources, blocks, pixels):
    return (
        jax.ShapeDtypeStruct((sources * blocks, pixels, DEPTH), BF16),
        jax.ShapeDtypeStruct((sources * blocks * blocks + 1, 4), jnp.int32),
    )


def own(info, right, payload):
    blocks, rows, pixels = payload.shape
    classes = rows - PART_ROWS
    return pl.pallas_call(
        own_body,
        out_shape=(
            jax.ShapeDtypeStruct((blocks, classes, pixels), F32),
            jax.ShapeDtypeStruct((1,), jnp.int32),
            *plan_shapes(1, blocks, pixels),
        ),
        in_specs=[SMEM, VMEM, VMEM],
        out_specs=(VMEM, SMEM, VMEM, SMEM),
        scratch_shapes=[pltpu.VMEM((blocks, classes, pixels), BF16), *buffers(pixels)],
        compiler_params=PARAMS,
        cost_estimate=stage_cost(2, pixels),
        name="own",
    )(info, right, payload)


def again_body(count_src, first, ending, *refs):
    refs = list(refs)
    right_ref, left, jobs = refs[:3]
    sources = refs[3 : 3 + count_src]
    del refs[: 3 + count_src]
    if ending:
        unary_ref, compat_ref = refs[:2]
        del refs[:2]
    total_in = None if first else refs.pop(0)
    total_ref, token_ref, *bufs = refs
    total = bufs.pop() if ending else total_ref
    probs = sources[0] if count_src == 1 else bufs.pop()
    blocks = total.shape[0]
    token_ref[0] = jobs[0, 0]
    bufs[-1][...] = jnp.zeros_like(bufs[-1])
    for block in range(blocks):
        total[block] = -sources[0][block].astype(F32) if first else total_in[block]
        if count_src > 1:
            for index in range(count_src):
                probs[index * blocks + block] = sources[index][block]
    sweep(jobs, left, right_ref, probs, bufs, total)
    if ending:
        for block in range(blocks):
            total_ref[block] = finish(unary_ref, compat_ref, total[block], block)


def again(right, plan, sources, total, ending):
    blocks, classes, pixels = sources[0].shape
    number = len(sources)
    first = total is None
    operands = [right, *plan, *sources, *ending]
    specs = [VMEM, VMEM, SMEM] + [VMEM] * (number + len(ending))
    if not first:
        operands.append(total)
        specs.append(VMEM)
    scratch = buffers(pixels)
    if number > 1:
        scratch.append(pltpu.VMEM((number * blocks, classes, pixels), BF16))
    if ending:
        scratch.append(pltpu.VMEM((blocks, classes, pixels), F32))
    return pl.pallas_call(
        functools.partial(again_body, number, first, bool(ending)),
        out_shape=(
            jax.ShapeDtypeStruct((blocks, classes, pixels), F32),
            jax.ShapeDtypeStruct((1,), jnp.int32),
        ),
        in_specs=specs,
        out_specs=(VMEM, SMEM),
        scratch_shapes=scratch,
        compiler_params=PARAMS,
        cost_estimate=stage_cost(2 if first else number, pixels),
        name="own_again" if first else "remote_again",
    )(*operands)


def remote_body(stage, ending, *refs):
    refs = list(refs)
    info_ref, right_ref = refs[:2]
    payloads = refs[2 : 2 + len(stage)]
    del refs[: 2 + len(stage)]
    if ending:
        unary_ref, compat_ref = refs[:2]
        del refs[:2]
    total_in, total_ref, token_ref, left, jobs, probs, *bufs = refs
    total = bufs.pop() if ending else total_ref
    blocks, classes, pixels = total.shape
    slots = slots_of(info_ref)

    clear(jobs, bufs)
    for block in range(blocks):
        total[block] = total_in[block]

    for index, (source, payload_ref) in enumerate(zip(stage, payloads)):
        offset = info_ref[3 * slots + 1 + source]
        packed = meta_counts(payload_ref, classes, blocks, offset)

        def multiplicity(block, target):
            ahead = jnp.int32(0)
            for slot in range(slots):
                owner, distance, partner = slot_of(info_ref, slots, slot)
                hit = (owner == target) & (distance == offset) & (partner == block)
                ahead = ahead + jnp.where(hit & is_live(info_ref, slots, slot), 1, 0)
            behind = lax.shift_right_logical(packed, 3 * (block * blocks + target)) & 7
            return jnp.where(offset > 0, ahead, behind)

        @pl.loop(0, blocks)
        def _(block):
            counts = [multiplicity(block, target) for target in range(blocks)]
            for target in range(blocks):
                @pl.when(counts[target] > 0)
                def _():
                    entry = jobs[0, 0] + 1
                    jobs[0, 0] = entry
                    jobs[entry, 1] = index * blocks + block
                    jobs[entry, 2] = target
                    jobs[entry, 3] = counts[target]

            @pl.when(sum(counts) > 0)
            def _():
                left[index * blocks + block] = left_operand(payload_ref, block, classes)
                probs[index * blocks + block] = payload_ref[block, :classes, :]

    token_ref[0] = jobs[0, 0]
    sweep(jobs, left, right_ref, probs, bufs, total)

    if ending:
        for block in range(blocks):
            result = finish(unary_ref, compat_ref, total[block], block)
            total_ref[block] = result.astype(total_ref.dtype)


def remote(stage, info, right, payloads, total, ending):
    blocks, classes, pixels = total.shape
    number = len(stage)
    operands = [info, right, *payloads, *ending, total]
    scratch = [pltpu.VMEM((number * blocks, classes, pixels), BF16), *buffers(pixels)]
    if ending:
        scratch.append(pltpu.VMEM((blocks, classes, pixels), F32))
    return pl.pallas_call(
        functools.partial(remote_body, stage, bool(ending)),
        out_shape=(
            jax.ShapeDtypeStruct((blocks, classes, pixels), BF16 if ending else F32),
            jax.ShapeDtypeStruct((1,), jnp.int32),
            *plan_shapes(number, blocks, pixels),
        ),
        in_specs=[SMEM] + [VMEM] * (len(operands) - 1),
        out_specs=(VMEM, SMEM, VMEM, SMEM),
        scratch_shapes=scratch,
        compiler_params=PARAMS,
        cost_estimate=stage_cost(number, pixels),
        name="remote",
    )(*operands)


def pick_body(flag_ref, even_ref, odd_ref, after_ref, out_ref):
    @pl.when(flag_ref[0] == 1)
    def _():
        out_ref[...] = even_ref[...]

    @pl.when(flag_ref[0] != 1)
    def _():
        out_ref[...] = odd_ref[...]


def pick(flag, even, odd, after):
    return pl.pallas_call(
        pick_body,
        out_shape=jax.ShapeDtypeStruct(even.shape, even.dtype),
        in_specs=[SMEM, VMEM, VMEM, SMEM],
        out_specs=VMEM,
        compiler_params=SMALL,
        name="pick",
    )(flag, even, odd, after)


def gate_body(value_ref, after_ref, out_ref):
    out_ref[...] = value_ref[...]


def gate(value, after):
    return pl.pallas_call(
        gate_body,
        out_shape=jax.ShapeDtypeStruct(value.shape, value.dtype),
        in_specs=[VMEM, SMEM],
        out_specs=VMEM,
        compiler_params=SMALL,
        name="gate",
    )(value, after)


def permute(value, place):
    count = lax.axis_size("rows")
    moves = [(index, place(index)) for index in range(count)]
    return lax.ppermute(value, "rows", [move for move in moves if 0 <= move[1] < count])


def other_core(value):
    return permute(value, lambda index: index ^ 1)


def even_pair(value):
    return permute(value, lambda index: index ^ 2)


def next_pair(value):
    return permute(value, lambda index: index - 4 if index & 2 else index + 4)


def on_device(unary, features, compat, pairs, pair_count):
    blocks = unary.shape[0]
    me = lax.axis_index("rows")
    core, side = me & 1, (me >> 1) & 1
    off_core = 1 - 2 * core
    off_even = 2 - 4 * side
    offsets = jnp.stack([jnp.zeros_like(off_core), off_core, off_even, -off_even, -off_core])
    info = jnp.concatenate([pairs[0], pairs[1], pairs[2], pair_count, offsets.astype(jnp.int32)])
    payload, right = prep(unary, jnp.transpose(features, (1, 0, 2)), info)
    take_even = (core == side).astype(jnp.int32).reshape(1)
    plans = {}

    def first_stage(stage, sources, total, ending=()):
        if total is None:
            total, token, *plans[stage] = own(info, right, *sources)
        else:
            total, token, *plans[stage] = remote(stage, info, right, sources, total, ending)
        return total, token

    def later_stage(stage, sources, total, ending=()):
        return again(right, plans[stage], sources, total, ending)

    def run(value, advance):
        core_value = other_core(value)
        even_value = even_pair(value)
        total, token = advance((0,), [value], None)
        odd_value = next_pair(gate(even_value, token))
        total, token = advance((1, 2), [core_value, even_value], total)
        far_value = other_core(pick(take_even, even_value, odd_value, token))
        total, token = advance((3,), [odd_value], total)
        total, token = advance((4,), [far_value], total, (unary, compat))
        return total

    return run(run(payload, first_stage), later_stage)


def solution(mesh):
    placed = (
        P(("groups", "rows"), None, None),
        P(("groups", "rows"), None, None),
        P(),
        P(None, ("groups", "rows")),
        P(("groups", "rows")),
    )
    return jax.shard_map(
        on_device,
        mesh=mesh,
        in_specs=placed,
        out_specs=P(("groups", "rows"), None, None),
        check_vma=False,
    )
```

```python
import functools

import jax
import jax.numpy as jnp
from jax import lax
from jax.experimental import pallas as pl
from jax.experimental.pallas import tpu as pltpu
from jax.sharding import PartitionSpec as P

ITERS = 2
FEATS = 5
PART_ROWS = 16
META = 3 * FEATS
DEPTH = 4 * PART_ROWS
ROWS = 256
SPAN = 512
RING = 4
LOG2E = 1.4426950408889634
F32 = jnp.float32
BF16 = jnp.bfloat16
VMEM = pl.BlockSpec(memory_space=pltpu.VMEM)
SMEM = pl.BlockSpec(memory_space=pltpu.SMEM)
ANY = pl.BlockSpec(memory_space=pl.ANY)
PARAMS = pltpu.CompilerParams(vmem_limit_bytes=20 * 2**20)
SMALL = pltpu.CompilerParams(vmem_limit_bytes=16 * 2**20)


def split3(value):
    high = value.astype(BF16)
    rest = value - high.astype(F32)
    middle = rest.astype(BF16)
    low = (rest - middle.astype(F32)).astype(BF16)
    return high, middle, low


def softmax(scores):
    shifted = jnp.exp(scores - jnp.max(scores, axis=0, keepdims=True))
    return shifted / jnp.sum(shifted, axis=0, keepdims=True)


def small_dot(left, right):
    return jnp.dot(left, right, preferred_element_type=F32)


def slot_of(info_ref, slots, slot):
    return [info_ref[part * slots + slot] for part in range(3)]


def slots_of(info_ref):
    return (info_ref.shape[0] - 6) // 3


def is_live(info_ref, slots, slot):
    return slot < info_ref[3 * slots]


def slot_code(info_ref, slots, slot):
    owner, offset, partner = slot_of(info_ref, slots, slot)
    return owner * 6 + offset * 2 + partner


def norm_parts(values):
    norm = jnp.sum(values * values, axis=0, keepdims=True) * (-0.5 * LOG2E)
    return [part.astype(F32) for part in split3(norm)]


def prep_body(unary_ref, feat_ref, info_ref, payload_ref, right_ref):
    blocks, classes, pixels = unary_ref.shape
    slots = slots_of(info_ref)
    row = lax.broadcasted_iota(jnp.int32, (PART_ROWS, 8), 0)
    col = lax.broadcasted_iota(jnp.int32, (PART_ROWS, 8), 1)
    place = [
        jnp.where((row == col + FEATS * part) & (col < FEATS), 1.0, 0.0).astype(BF16)
        for part in range(3)
    ]
    spread = place[0] + place[1] + place[2]
    wide_row = lax.broadcasted_iota(jnp.int32, (PART_ROWS, pixels), 0)
    wide_col = lax.broadcasted_iota(jnp.int32, (PART_ROWS, pixels), 1)
    feat_row = lax.broadcasted_iota(jnp.int32, (8, pixels), 0)
    meta = jnp.zeros((PART_ROWS, pixels), F32)
    for slot in range(slots):
        code = jnp.where(is_live(info_ref, slots, slot), slot_code(info_ref, slots, slot), -1)
        meta = meta + jnp.where((wide_row == META) & (wide_col == code), 1.0, 0.0)
    for block in range(blocks):
        payload_ref[block, :classes, :] = softmax(-unary_ref[block]).astype(BF16)
        values = jnp.zeros((8, pixels), F32)
        for feature in range(FEATS):
            values = jnp.where(feat_row == feature, feat_ref[feature, block : block + 1, :], values)
        parts = split3(values)
        own = meta
        for part in range(3):
            own = own + small_dot(place[part], parts[part])
        payload_ref[block, classes:, :] = own.astype(BF16)
        for index, part in enumerate(split3(values * LOG2E)):
            right_ref[block, index * PART_ROWS : (index + 1) * PART_ROWS, :] = small_dot(
                spread, part
            ).astype(BF16)
        high, middle, low = norm_parts(values)
        norms = jnp.where(wide_row < 3, 1.0, 0.0)
        for index, part in enumerate((high, middle, low)):
            norms = jnp.where(wide_row == 3 + index, part, norms)
        right_ref[block, 3 * PART_ROWS :, :] = norms.astype(BF16)


def prep(unary, feats, info):
    blocks, classes, pixels = unary.shape
    return pl.pallas_call(
        prep_body,
        out_shape=(
            jax.ShapeDtypeStruct((blocks, classes + PART_ROWS, pixels), BF16),
            jax.ShapeDtypeStruct((blocks, DEPTH, pixels), BF16),
        ),
        in_specs=[VMEM, VMEM, SMEM],
        out_specs=(VMEM, VMEM),
        compiler_params=SMALL,
        name="prep",
    )(unary, feats, info)


def left_operand(payload_ref, block, classes):
    pixels = payload_ref.shape[2]
    own = payload_ref[block, classes:, :]
    row = lax.broadcasted_iota(jnp.int32, (8, PART_ROWS), 0)
    col = lax.broadcasted_iota(jnp.int32, (8, PART_ROWS), 1)
    gather = (row < FEATS) & ((col == row) | (col == row + FEATS) | (col == row + 2 * FEATS))
    values = small_dot(jnp.where(gather, 1.0, 0.0).astype(BF16), own)
    wide_row = lax.broadcasted_iota(jnp.int32, (PART_ROWS, pixels), 0)
    norms = jnp.where((wide_row >= 3) & (wide_row < 6), 1.0, 0.0)
    for index, part in enumerate(norm_parts(values)):
        norms = jnp.where(wide_row == index, part, norms)
    return jnp.concatenate([own, own, own, norms.astype(BF16)], axis=0).T


def meta_counts(payload_ref, classes, blocks, offset):
    row = lax.broadcasted_iota(jnp.int32, (PART_ROWS, 128), 0)
    col = lax.broadcasted_iota(jnp.int32, (PART_ROWS, 128), 1)
    own = payload_ref[0, classes:, :128].astype(F32)
    weight = jnp.zeros((PART_ROWS, 128), F32)
    for block in range(blocks):
        for target in range(blocks):
            lane = block * 6 - offset * 2 + target
            step = 8.0 ** (block * blocks + target)
            weight = jnp.where((row == META) & (col == lane), step, weight)
    return jnp.sum(own * weight).astype(jnp.int32)


def finish(unary_ref, compat_ref, message, block):
    scale = 16.0 / unary_ref.shape[2]
    pairwise = jnp.dot(
        compat_ref[...], message, precision=lax.Precision.HIGHEST, preferred_element_type=F32
    )
    return softmax(-unary_ref[block] - pairwise * scale)


def cuts_of(pixels):
    return [slice(start, start + SPAN) for start in range(0, pixels, SPAN)]


def rows_of(chunk):
    return slice(chunk * ROWS, (chunk + 1) * ROWS)


def local_count(info_ref, slots):
    count = jnp.int32(0)
    for slot in range(slots):
        hit = is_live(info_ref, slots, slot) & (slot_of(info_ref, slots, slot)[1] == 0)
        count = count + jnp.where(hit, 1, 0)
    return count


def sweep(jobs, left, right_ref, probs, bufs, total):
    pixels = right_ref.shape[2]
    chunks = pixels // ROWS
    number = jobs[0, 0]

    def product(entry, chunk, cut):
        index, target, count = entry
        share = jnp.dot(
            probs[index, :, rows_of(chunk)],
            bufs[chunk % RING][:, cut],
            preferred_element_type=F32,
        )
        total[target, :, cut] += count.astype(F32) * share

    @pl.loop(0, number)
    def _(job):
        entry = index, target, count = [jobs[job + 1, column] for column in range(1, 4)]
        earlier = [jobs[job, column] for column in range(1, 4)]
        for chunk in range(chunks):
            for cut in cuts_of(pixels):
                scores = jnp.dot(
                    left[index, rows_of(chunk), :], right_ref[target, :, cut], preferred_element_type=F32
                )
                bufs[chunk % RING][:, cut] = jnp.exp2(scores).astype(BF16)
                if chunk > 0:
                    product(entry, chunk - 1, cut)
                else:
                    product(earlier, chunks - 1, cut)

    @pl.when(number > 0)
    def _():
        entry = [jobs[number, column] for column in range(1, 4)]
        for cut in cuts_of(pixels):
            product(entry, chunks - 1, cut)


def clear(jobs, bufs):
    for column in range(4):
        jobs[0, column] = 0
    bufs[-1][...] = jnp.zeros_like(bufs[-1])


def own_body(info_ref, right_ref, payload_ref, total_ref, token_ref, left, jobs, probs, *bufs):
    blocks, classes, pixels = total_ref.shape
    slots = slots_of(info_ref)
    count = local_count(info_ref, slots)
    token_ref[0] = count
    clear(jobs, bufs)
    for block in range(blocks):
        total_ref[block] = -payload_ref[block, :classes, :].astype(F32)
        probs[block] = payload_ref[block, :classes, :]
        left[block] = left_operand(payload_ref, block, classes)
    pairs = [(block, target) for block in range(blocks) for target in range(blocks)]
    for number, (block, target) in enumerate(sorted(pairs, key=lambda pair: pair[0] != pair[1])):
        jobs[number + 1, 1] = block
        jobs[number + 1, 2] = target
        jobs[number + 1, 3] = 1 if block == target else count
    jobs[0, 0] = jnp.where(count > 0, blocks * blocks, blocks)
    sweep(jobs, left, right_ref, probs, bufs, total_ref)


def buffers(pixels):
    return [pltpu.VMEM((ROWS, pixels), BF16) for ring in range(RING)]


def stage_cost(sources, pixels):
    return pl.CostEstimate(
        flops=2 * 2 * sources * pixels * pixels * 640, bytes_accessed=2**22, transcendentals=0
    )


def plan_shapes(sources, blocks, pixels):
    return (
        jax.ShapeDtypeStruct((sources * blocks, pixels, DEPTH), BF16),
        jax.ShapeDtypeStruct((sources * blocks * blocks + 1, 4), jnp.int32),
    )


def own(info, right, payload):
    blocks, rows, pixels = payload.shape
    classes = rows - PART_ROWS
    return pl.pallas_call(
        own_body,
        out_shape=(
            jax.ShapeDtypeStruct((blocks, classes, pixels), F32),
            jax.ShapeDtypeStruct((1,), jnp.int32),
            *plan_shapes(1, blocks, pixels),
        ),
        in_specs=[SMEM, VMEM, VMEM],
        out_specs=(VMEM, SMEM, VMEM, SMEM),
        scratch_shapes=[pltpu.VMEM((blocks, classes, pixels), BF16), *buffers(pixels)],
        compiler_params=PARAMS,
        cost_estimate=stage_cost(2, pixels),
        name="own",
    )(info, right, payload)


def again_body(count_src, first, ending, *refs):
    refs = list(refs)
    right_ref, left, jobs = refs[:3]
    sources = refs[3 : 3 + count_src]
    del refs[: 3 + count_src]
    if ending:
        unary_ref, compat_ref = refs[:2]
        del refs[:2]
    total_in = None if first else refs.pop(0)
    total_ref, token_ref, *bufs = refs
    total = bufs.pop() if ending else total_ref
    probs = sources[0] if count_src == 1 else bufs.pop()
    blocks = total.shape[0]
    token_ref[0] = jobs[0, 0]
    bufs[-1][...] = jnp.zeros_like(bufs[-1])
    for block in range(blocks):
        total[block] = -sources[0][block].astype(F32) if first else total_in[block]
        if count_src > 1:
            for index in range(count_src):
                probs[index * blocks + block] = sources[index][block]
    sweep(jobs, left, right_ref, probs, bufs, total)
    if ending:
        for block in range(blocks):
            total_ref[block] = finish(unary_ref, compat_ref, total[block], block)


def again(right, plan, sources, total, ending):
    blocks, classes, pixels = sources[0].shape
    number = len(sources)
    first = total is None
    operands = [right, *plan, *sources, *ending]
    specs = [VMEM, VMEM, SMEM] + [VMEM] * (number + len(ending))
    if not first:
        operands.append(total)
        specs.append(VMEM)
    scratch = buffers(pixels)
    if number > 1:
        scratch.append(pltpu.VMEM((number * blocks, classes, pixels), BF16))
    if ending:
        scratch.append(pltpu.VMEM((blocks, classes, pixels), F32))
    return pl.pallas_call(
        functools.partial(again_body, number, first, bool(ending)),
        out_shape=(
            jax.ShapeDtypeStruct((blocks, classes, pixels), F32),
            jax.ShapeDtypeStruct((1,), jnp.int32),
        ),
        in_specs=specs,
        out_specs=(VMEM, SMEM),
        scratch_shapes=scratch,
        compiler_params=PARAMS,
        cost_estimate=stage_cost(2 if first else number, pixels),
        name="own_again" if first else "remote_again",
    )(*operands)


def remote_body(stage, ending, *refs):
    refs = list(refs)
    info_ref, right_ref = refs[:2]
    payloads = refs[2 : 2 + len(stage)]
    del refs[: 2 + len(stage)]
    if ending:
        unary_ref, compat_ref = refs[:2]
        del refs[:2]
    total_in, total_ref, token_ref, left, jobs, probs, *bufs = refs
    total = bufs.pop() if ending else total_ref
    blocks, classes, pixels = total.shape
    slots = slots_of(info_ref)

    clear(jobs, bufs)
    for block in range(blocks):
        total[block] = total_in[block]

    for index, (source, payload_ref) in enumerate(zip(stage, payloads)):
        offset = info_ref[3 * slots + 1 + source]
        packed = meta_counts(payload_ref, classes, blocks, offset)

        def multiplicity(block, target):
            ahead = jnp.int32(0)
            for slot in range(slots):
                owner, distance, partner = slot_of(info_ref, slots, slot)
                hit = (owner == target) & (distance == offset) & (partner == block)
                ahead = ahead + jnp.where(hit & is_live(info_ref, slots, slot), 1, 0)
            behind = lax.shift_right_logical(packed, 3 * (block * blocks + target)) & 7
            return jnp.where(offset > 0, ahead, behind)

        @pl.loop(0, blocks)
        def _(block):
            counts = [multiplicity(block, target) for target in range(blocks)]
            for target in range(blocks):
                @pl.when(counts[target] > 0)
                def _():
                    entry = jobs[0, 0] + 1
                    jobs[0, 0] = entry
                    jobs[entry, 1] = index * blocks + block
                    jobs[entry, 2] = target
                    jobs[entry, 3] = counts[target]

            @pl.when(sum(counts) > 0)
            def _():
                left[index * blocks + block] = left_operand(payload_ref, block, classes)
                probs[index * blocks + block] = payload_ref[block, :classes, :]

    token_ref[0] = jobs[0, 0]
    sweep(jobs, left, right_ref, probs, bufs, total)

    if ending:
        for block in range(blocks):
            result = finish(unary_ref, compat_ref, total[block], block)
            total_ref[block] = result.astype(total_ref.dtype)


def remote(stage, info, right, payloads, total, ending):
    blocks, classes, pixels = total.shape
    number = len(stage)
    operands = [info, right, *payloads, *ending, total]
    scratch = [pltpu.VMEM((number * blocks, classes, pixels), BF16), *buffers(pixels)]
    if ending:
        scratch.append(pltpu.VMEM((blocks, classes, pixels), F32))
    return pl.pallas_call(
        functools.partial(remote_body, stage, bool(ending)),
        out_shape=(
            jax.ShapeDtypeStruct((blocks, classes, pixels), BF16 if ending else F32),
            jax.ShapeDtypeStruct((1,), jnp.int32),
            *plan_shapes(number, blocks, pixels),
        ),
        in_specs=[SMEM] + [VMEM] * (len(operands) - 1),
        out_specs=(VMEM, SMEM, VMEM, SMEM),
        scratch_shapes=scratch,
        compiler_params=PARAMS,
        cost_estimate=stage_cost(number, pixels),
        name="remote",
    )(*operands)


def pick_body(flag_ref, even_ref, odd_ref, after_ref, out_ref):
    @pl.when(flag_ref[0] == 1)
    def _():
        out_ref[...] = even_ref[...]

    @pl.when(flag_ref[0] != 1)
    def _():
        out_ref[...] = odd_ref[...]


def pick(flag, even, odd, after):
    return pl.pallas_call(
        pick_body,
        out_shape=jax.ShapeDtypeStruct(even.shape, even.dtype),
        in_specs=[SMEM, VMEM, VMEM, SMEM],
        out_specs=VMEM,
        compiler_params=SMALL,
        name="pick",
    )(flag, even, odd, after)


def gate_body(value_ref, after_ref, out_ref):
    pass


def gate(value, after):
    return pl.pallas_call(
        gate_body,
        out_shape=jax.ShapeDtypeStruct(value.shape, value.dtype),
        in_specs=[ANY, SMEM],
        out_specs=ANY,
        input_output_aliases={0: 0},
        compiler_params=SMALL,
        name="gate",
    )(value, after)


def permute(value, place):
    count = lax.axis_size("rows")
    moves = [(index, place(index)) for index in range(count)]
    return lax.ppermute(value, "rows", [move for move in moves if 0 <= move[1] < count])


def other_core(value):
    return permute(value, lambda index: index ^ 1)


def even_pair(value):
    return permute(value, lambda index: index ^ 2)


def next_pair(value):
    return permute(value, lambda index: index - 4 if index & 2 else index + 4)


def on_device(unary, features, compat, pairs, pair_count):
    blocks = unary.shape[0]
    me = lax.axis_index("rows")
    core, side = me & 1, (me >> 1) & 1
    off_core = 1 - 2 * core
    off_even = 2 - 4 * side
    offsets = jnp.stack([jnp.zeros_like(off_core), off_core, off_even, -off_even, -off_core])
    info = jnp.concatenate([pairs[0], pairs[1], pairs[2], pair_count, offsets.astype(jnp.int32)])
    payload, right = prep(unary, jnp.transpose(features, (1, 0, 2)), info)
    take_even = (core == side).astype(jnp.int32).reshape(1)
    plans = {}

    def first_stage(stage, sources, total, ending=()):
        if total is None:
            total, token, *plans[stage] = own(info, right, *sources)
        else:
            total, token, *plans[stage] = remote(stage, info, right, sources, total, ending)
        return total, token

    def later_stage(stage, sources, total, ending=()):
        return again(right, plans[stage], sources, total, ending)

    def run(value, advance):
        core_value = other_core(value)
        even_value = even_pair(value)
        total, token = advance((0,), [value], None)
        even_value = gate(even_value, token)
        odd_value = next_pair(even_value)
        total, token = advance((1, 2), [core_value, even_value], total)
        far_value = other_core(pick(take_even, even_value, odd_value, token))
        total, token = advance((3,), [odd_value], total)
        total, token = advance((4,), [far_value], total, (unary, compat))
        return total

    return run(run(payload, first_stage), later_stage)


def solution(mesh):
    placed = (
        P(("groups", "rows"), None, None),
        P(("groups", "rows"), None, None),
        P(),
        P(None, ("groups", "rows")),
        P(("groups", "rows")),
    )
    return jax.shard_map(
        on_device,
        mesh=mesh,
        in_specs=placed,
        out_specs=P(("groups", "rows"), None, None),
        check_vma=False,
    )
```
